32 devices in a mesh: grp: 2 (over y), dap: 4 (over z), sub: 2 (over x), pair: 2 (over core).
Axes of the slice: x: 2, y: 2, z: 4, core: 2. Of those that a mesh axis runs over, the one named last changes fastest.
Arguments:
- pair_input: bfloat16 [320, 160, 128], P(('grp', 'dap'), ('sub', 'pair')), parts along dimension 0, may hold values from -6 to 6
- residue_mask: int32 [320], P('grp'), parts along dimension 0, may hold values 0 or 1
- entry_gain: float32 [2, 128], replicated, may hold values from 0.5 to 1.5
- input_weight: bfloat16 [2, 128, 640], replicated, may hold values from -0.5 to 0.5
- middle_gain: float32 [2, 128], replicated, may hold values from 0.5 to 1.5
- output_weight: bfloat16 [2, 128, 128], replicated, may hold values from -0.5 to 0.5
- final_gain: float32 [128], replicated, may hold values from 0.5 to 1.5
- expand_weight: bfloat16 [128, 512], replicated, may hold values from -0.5 to 0.5
- shrink_weight: bfloat16 [512, 128], replicated, may hold values from -0.25 to 0.25
Outputs:
- pair_output: bfloat16 [320, 160, 128], P(('grp', 'dap'), ('sub', 'pair')), parts along dimension 0
The draws below stay inside these ranges and needn't reach their ends.
There are 2 independent parts, one for each index of `grp`. The reference program is written for one: setup_inputs(seed, part) draws one part's arguments, and reference() takes and returns one part's arrays. A program takes and returns all parts, laid end to end along the dimension named above; an argument that names none is the same for every part. Nothing has to cross between parts.
All inputs are finite; a program needn't handle non-finite values.
Results may differ from the reference program's by a relative error of at most 0.012.
Values may be sent and summed in bfloat16 or wider, within the bound.
No kernel may reach another device: no remote copies, remote signals or barrier semaphores. Data moves between devices by JAX's collectives and lax.ppermute only.
A program may use at most 64 MiB of HBM per device.

```python
import jax
import jax.numpy as jnp
from jax import lax

C = 128
H = 128
F = 512
N = 160


def with_ends(array, stream_key, least, high):
    longest = array.shape.index(max(array.shape))
    spots = []
    for shift in (0, 1):
        where = [jax.random.randint(jax.random.fold_in(stream_key, axis), (), 0, length) for axis, length in enumerate(array.shape)]
        where[longest] = (where[longest] + shift) % array.shape[longest]
        spots.append(tuple(where))
    return array.at[spots[0]].set(least).at[spots[1]].set(high)


def levels(own_key, shape, shards, least, high):
    factor_of, own = 1.0, jax.random.fold_in(own_key, 6)
    for dim, shards_of in shards:
        heights = jnp.exp(jax.random.uniform(jax.random.fold_in(own, dim), (shards_of,), jnp.float32, least / len(shards), high / len(shards)))
        factor_of = factor_of * jnp.repeat(heights, shape[dim] // shards_of).reshape([-1 if axis == dim else 1 for axis in range(len(shape))])
    return factor_of


def noise(rng, extent, width, reach, split=(), held_as=jnp.bfloat16):
    array = width * jax.random.normal(rng, extent, jnp.float32)
    if split:
        array = array * levels(rng, extent, split, -0.22, 0.18)
    return jnp.clip(array, -reach, reach).astype(held_as)


def setup_inputs(seed: int = 0, part: int = 0) -> dict:
    key_of = jax.random.split(jax.random.key(seed), 10)
    part_splits = jax.random.split(jax.random.fold_in(key_of[9], part), 10)
    return {
        "pair_input": noise(part_splits[0], (N, N, C), 1.0, 6.0, ((0, 4), (1, 4))),
        "residue_mask": with_ends((jax.random.randint(part_splits[1], (N,), 0, 8) < 7).astype(jnp.int32), jax.random.fold_in(part_splits[1], 1), 0, 1),
        "entry_gain": jnp.clip(jax.random.uniform(key_of[2], (2, C), jnp.float32, 0.5, 1.5), 0.5, 1.5),
        "input_weight": noise(key_of[3], (2, C, 4 * H + C), C ** -0.5, 0.5),
        "middle_gain": jnp.clip(jax.random.uniform(key_of[4], (2, H), jnp.float32, 0.5, 1.5), 0.5, 1.5),
        "output_weight": noise(key_of[5], (2, H, C), H ** -0.5, 0.5),
        "final_gain": jnp.clip(jax.random.uniform(key_of[6], (C,), jnp.float32, 0.5, 1.5), 0.5, 1.5),
        "expand_weight": noise(key_of[7], (C, F), C ** -0.5, 0.5),
        "shrink_weight": noise(key_of[8], (F, C), F ** -0.5, 0.25),
    }


def layer_norm(values, factor, dimension):
    average = lax.optimization_barrier(jnp.mean(values, axis=dimension, keepdims=True))
    centred = values - average
    variance = lax.optimization_barrier(jnp.mean(centred * centred, axis=dimension, keepdims=True))
    return centred * lax.rsqrt(variance + 1e-05) * factor

def triangle_update(stream, pair_mask, entry_gain, input_weight, middle_gain, output_weight, incoming):
    length = stream.shape[0]
    channels = stream.shape[2]
    hidden = output_weight.shape[0]
    normed = layer_norm(stream, entry_gain, 2).astype(jnp.bfloat16).reshape(length * length, channels)

    def project(column_from, column_to):
        product = jnp.dot(normed, input_weight[:, column_from:column_to], preferred_element_type=jnp.float32)
        return product.reshape(length, length, column_to - column_from)
    left_side = (pair_mask * jax.nn.sigmoid(project(hidden, 2 * hidden)) * project(0, hidden)).astype(jnp.bfloat16)
    right_side = (pair_mask * jax.nn.sigmoid(project(3 * hidden, 4 * hidden)) * project(2 * hidden, 3 * hidden)).astype(jnp.bfloat16)
    gate_vals = jax.nn.sigmoid(project(4 * hidden, 4 * hidden + channels))
    left_major = jnp.moveaxis(left_side, 2, 0).astype(jnp.float32)
    right_major = jnp.moveaxis(right_side, 2, 0).astype(jnp.float32)
    if incoming:
        summed = jnp.einsum('cki,ckj->cij', left_major, right_major, precision=lax.Precision.HIGHEST)
    else:
        summed = jnp.einsum('cik,cjk->cij', left_major, right_major, precision=lax.Precision.HIGHEST)
    mixed_sum = jnp.moveaxis(summed, 0, 2).astype(jnp.bfloat16)
    middle = layer_norm(mixed_sum.astype(jnp.float32), middle_gain, 2).astype(jnp.bfloat16)
    output = jnp.dot(middle.reshape(length * length, hidden), output_weight, preferred_element_type=jnp.float32)
    return stream + gate_vals * output.reshape(length, length, channels)

def reference(pair_input, residue_mask, entry_gain, input_weight, middle_gain, output_weight, final_gain, expand_weight, shrink_weight):
    mask_values = residue_mask.astype(jnp.float32)
    pair_mask = (mask_values[:, None] * mask_values[None, :])[:, :, None]
    stream = pair_input.astype(jnp.float32)
    for update_id in range(2):
        stream = triangle_update(stream, pair_mask, entry_gain[update_id], input_weight[update_id], middle_gain[update_id], output_weight[update_id], update_id == 1)

    def finish(row_stream):
        normed = layer_norm(row_stream, final_gain, 1).astype(jnp.bfloat16)
        expanded = jax.nn.relu(jnp.dot(normed, expand_weight, preferred_element_type=jnp.float32)).astype(jnp.bfloat16)
        return (row_stream + jnp.dot(expanded, shrink_weight, preferred_element_type=jnp.float32)).astype(jnp.bfloat16)
    return lax.map(finish, stream)
```

```python
import functools

import jax
import jax.numpy as jnp
from jax import lax
from jax.experimental import pallas as pl
from jax.experimental.pallas import tpu as pltpu
from jax.sharding import PartitionSpec as P

F32 = jnp.float32
BF16 = jnp.bfloat16
LANES = 128
GROUP = 8
CHIPS = ("dap", "sub", "pair")


def layer_norm(values, factor, dimension):
    average = jnp.mean(values, axis=dimension, keepdims=True)
    centred = values - average
    variance = jnp.mean(centred * centred, axis=dimension, keepdims=True)
    return centred * lax.rsqrt(variance + 1e-05) * factor


def spread_rows(left_side, right_side):
    return (
        lax.all_to_all(left_side, ("sub", "pair"), split_axis=0, concat_axis=2, tiled=True),
        lax.all_to_all(right_side, ("sub", "pair"), split_axis=0, concat_axis=2, tiled=True),
    )


def return_rows(mixed_sum):
    return lax.all_to_all(mixed_sum, ("sub", "pair"), split_axis=2, concat_axis=0, tiled=True)


def outgoing_rows(left_side, right_side):
    left_wide, right_wide = spread_rows(left_side, right_side)
    summed = jnp.einsum(
        "cik,cjk->cij",
        left_wide,
        lax.all_gather(right_wide, "dap", axis=1, tiled=True),
        preferred_element_type=jnp.float32,
    )
    return return_rows(summed.astype(jnp.bfloat16))


def incoming_rows(left_side, right_side):
    left_wide, right_wide = spread_rows(left_side, right_side)
    flipped = lax.all_to_all(left_wide, "dap", split_axis=2, concat_axis=1, tiled=True)
    summed = jnp.einsum(
        "cki,ckj->cij",
        flipped,
        lax.all_gather(right_wide, "dap", axis=1, tiled=True),
        preferred_element_type=jnp.float32,
    )
    return return_rows(summed.astype(jnp.bfloat16))


def triangle_update(
    stream, pair_mask, entry_gain, input_weight, middle_gain, output_weight, incoming
):
    row_count, col_count, channels = stream.shape
    hidden = output_weight.shape[0]
    normed = (
        layer_norm(stream, entry_gain, 2)
        .astype(jnp.bfloat16)
        .reshape(row_count * col_count, channels)
    )
    projected = lax.dot_general(
        input_weight[:, : 4 * hidden],
        normed,
        (((0,), (1,)), ((), ())),
        preferred_element_type=jnp.float32,
    )
    projected = projected.reshape(4 * hidden, row_count, col_count)
    left_side = (
        pair_mask * jax.nn.sigmoid(projected[hidden : 2 * hidden]) * projected[:hidden]
    ).astype(jnp.bfloat16)
    right_side = (
        pair_mask * jax.nn.sigmoid(projected[3 * hidden :]) * projected[2 * hidden : 3 * hidden]
    ).astype(jnp.bfloat16)
    gate_vals = jax.nn.sigmoid(
        jnp.dot(normed, input_weight[:, 4 * hidden :], preferred_element_type=jnp.float32)
    )
    mixed_sum = (
        incoming_rows(left_side, right_side) if incoming else outgoing_rows(left_side, right_side)
    )
    middle = layer_norm(mixed_sum.astype(jnp.float32), middle_gain[:, None, None], 0).astype(
        jnp.bfloat16
    )
    middle = middle.reshape(hidden, row_count * col_count)
    output = lax.dot_general(
        middle, output_weight, (((0,), (0,)), ((), ())), preferred_element_type=jnp.float32
    )
    return stream + (gate_vals * output).reshape(row_count, col_count, channels)


def general_device(
    pair_input,
    residue_mask,
    entry_gain,
    input_weight,
    middle_gain,
    output_weight,
    final_gain,
    expand_weight,
    shrink_weight,
):
    row_count, col_count, channels = pair_input.shape
    row_offset = lax.axis_index("dap") * row_count
    col_offset = lax.axis_index(("sub", "pair")) * col_count
    row_mask = lax.dynamic_slice_in_dim(residue_mask, row_offset, row_count).astype(jnp.float32)
    col_mask = lax.dynamic_slice_in_dim(residue_mask, col_offset, col_count).astype(jnp.float32)
    pair_mask = row_mask[:, None] * col_mask[None, :]
    stream = pair_input.astype(jnp.float32)
    for update_id in range(2):
        stream = triangle_update(
            stream,
            pair_mask,
            entry_gain[update_id],
            input_weight[update_id],
            middle_gain[update_id],
            output_weight[update_id],
            update_id == 1,
        )
    flat = stream.reshape(row_count * col_count, channels)
    normed = layer_norm(flat, final_gain, 1).astype(jnp.bfloat16)
    expanded = jax.nn.relu(
        jnp.dot(normed, expand_weight, preferred_element_type=jnp.float32)
    ).astype(jnp.bfloat16)
    result = flat + jnp.dot(expanded, shrink_weight, preferred_element_type=jnp.float32)
    return result.astype(jnp.bfloat16).reshape(row_count, col_count, channels)


def sigmoid(values):
    return 0.5 * jnp.tanh(0.5 * values) + 0.5


def norm_rows(values, factor):
    average = jnp.mean(values, axis=0, keepdims=True)
    centred = values - average
    variance = jnp.mean(centred * centred, axis=0, keepdims=True)
    return centred * lax.rsqrt(variance + 1e-05) * factor


def column_of(gain_row, width):
    square = jnp.broadcast_to(gain_row, (gain_row.shape[1], gain_row.shape[1])).T
    return jnp.concatenate([square] * (width // square.shape[1]), axis=1)


def lane_index():
    return lax.broadcasted_iota(jnp.int32, (GROUP, LANES), 1)


def split_group(chunk, width, lane):
    pieces = []
    for row in range(GROUP):
        first, offset = divmod(row * width, LANES)
        piece = chunk[:, first * LANES : (first + 1) * LANES]
        if offset:
            piece = pltpu.roll(piece, LANES - offset, 1)
            if offset + width > LANES:
                after = chunk[:, (first + 1) * LANES : (first + 2) * LANES]
                after = pltpu.roll(after, LANES - offset, 1)
                piece = jnp.where(lane < LANES - offset, piece, after)
        pieces.append(jnp.where(lane < width, piece, 0.0))
    return pieces


def join_group(pieces, width, lane):
    parts = []
    for part in range(GROUP * width // LANES):
        begin = part * LANES
        value = None
        for row in range(begin // width, (begin + LANES - 1) // width + 1):
            shift = row * width - begin
            piece = pieces[row]
            if shift % LANES:
                piece = pltpu.roll(piece, shift % LANES, 1)
            value = piece if value is None else jnp.where(lane >= shift, piece, value)
        parts.append(value)
    return jnp.concatenate(parts, axis=1)


def pick_rows(table, starts, size):
    return jnp.concatenate(
        [table[pl.ds(pl.multiple_of(start, GROUP), size), :] for start in starts], axis=0
    )


def side_weights(table, meta, incoming):
    core, chip = meta[0], meta[1]
    hidden = table.shape[0] // 5
    mine = hidden // 2
    count = 8 if incoming else 4
    size = mine // count
    picked = []
    for base in range(4):
        starts = [
            base * hidden + core * mine + size * ((chip & (count - 1)) ^ k) for k in range(count)
        ]
        picked.append(pick_rows(table, starts, size))
    return jnp.concatenate(picked, axis=0).astype(BF16)


def send_sides(normed, weights, mask, messages, lanes, incoming):
    quarter = weights.shape[0] // 4
    projected = jnp.dot(weights, normed, preferred_element_type=F32)
    left = mask * sigmoid(projected[quarter : 2 * quarter]) * projected[:quarter]
    right = mask * sigmoid(projected[3 * quarter :]) * projected[2 * quarter : 3 * quarter]
    count = 8 if incoming else 4
    size = quarter // count
    for k in range(count):
        rows = slice(k * size, (k + 1) * size)
        messages[k][:, lanes] = jnp.concatenate([left[rows], right[rows]], axis=0).astype(BF16)
        if not incoming:
            messages[4 + k][:, lanes] = right[rows].astype(BF16)


def first_kernel(meta, own, other, mask, gain, weight, *refs):
    stream, normed_out, *messages, both, table = refs
    core = meta[0]
    rows, cols, channels = own.shape
    both[:, pl.ds(pl.multiple_of(core * cols, GROUP), cols), :] = own[...].astype(F32)
    both[:, pl.ds(pl.multiple_of((1 - core) * cols, GROUP), cols), :] = other[...].astype(F32)
    table[...] = weight[0].astype(F32).T
    weights = side_weights(table, meta, False)
    width = GROUP * 2 * cols
    factor = column_of(gain[0:1, :], width)

    @pl.loop(0, rows // GROUP)
    def _(step):
        lanes = pl.ds(pl.multiple_of(step * width, LANES), width)
        values = both[pl.ds(step * GROUP, GROUP)].reshape(width, channels).T
        stream[:, lanes] = values
        normed = norm_rows(values, factor).astype(BF16)
        normed_out[:, lanes] = normed
        send_sides(normed, weights, mask[:, lanes], messages, lanes, False)


def gate_kernel(normed, weight, gate, *, update):
    channels = normed.shape[0]
    hidden = (weight.shape[2] - channels) // 4
    table = weight[update, :, 4 * hidden :].astype(F32).T.astype(BF16)
    gate[...] = sigmoid(jnp.dot(table, normed[...], preferred_element_type=F32))


def outgoing_kernel(meta, *refs, rows, width):
    messages, outs = refs[:8], refs[8:12]
    left, right, total = refs[12:]
    dap, sub = meta[1] >> 1, meta[1] & 1
    lane = lane_index()
    count = outs[0].shape[0]
    span = 2 * rows

    @pl.loop(0, rows // GROUP)
    def _(step):
        lanes = pl.ds(pl.multiple_of(step * GROUP * width, LANES), GROUP * width)
        for k in range(8):
            values = messages[k][:, lanes].astype(F32)
            source = dap ^ (k >> 1)
            half = (source >> 1) ^ sub
            near = (source & 1) * rows
            if k < 4:
                begin = ((k >> 1) & 1) * rows + step * GROUP
                for c in range(0, count, GROUP):
                    for i, piece in enumerate(split_group(values[c : c + GROUP], width, lane)):
                        left[k & 1, pl.ds(c * span + begin + i, GROUP, stride=span), :] = piece
                values = values[count:]
            begin = half * (count * span) + near + step * GROUP
            for c in range(0, count, GROUP):
                for i, piece in enumerate(split_group(values[c : c + GROUP], width, lane)):
                    right[k & 1, pl.ds(c * span + begin + i, GROUP, stride=span), :] = piece

    @pl.loop(0, count)
    def _(c):
        here = pl.ds(pl.multiple_of(c * span, GROUP), span)
        a = jnp.concatenate([left[0, here, :], left[1, here, :]], axis=1).astype(BF16)
        for half in range(2):
            there = pl.ds(pl.multiple_of(half * (count * span) + c * span, GROUP), span)
            b = jnp.concatenate([right[0, there, :], right[1, there, :]], axis=1).astype(BF16)
            total[half, here, 0:width] = lax.dot_general(
                a, b, (((1,), (1,)), ((), ())), preferred_element_type=F32
            )

    @pl.loop(0, rows // GROUP)
    def _(step):
        lanes = pl.ds(pl.multiple_of(step * GROUP * width, LANES), GROUP * width)
        for k in range(4):
            begin = (k >> 1) * rows + step * GROUP
            joined = []
            for c in range(0, count, GROUP):
                pieces = [
                    total[k & 1, pl.ds(c * span + begin + i, GROUP, stride=span), :]
                    for i in range(GROUP)
                ]
                joined.append(join_group(pieces, width, lane))
            outs[k][:, lanes] = jnp.concatenate(joined, axis=0).astype(BF16)


def incoming_kernel(meta, *refs, rows, width):
    messages, outs = refs[:8], refs[8:16]
    left, right, total = refs[16:]
    dap, sub = meta[1] >> 1, meta[1] & 1
    lane = lane_index()
    count = outs[0].shape[0]
    span = 4 * rows
    tall = 2 * LANES

    @pl.loop(0, rows // GROUP)
    def _(step):
        lanes = pl.ds(pl.multiple_of(step * GROUP * width, LANES), GROUP * width)
        for k in range(8):
            values = messages[k][:, lanes].astype(F32)
            begin = (k >> 1) * rows + step * GROUP
            for side, part in ((left, values[:count]), (right, values[count:])):
                for i, piece in enumerate(split_group(part, width, lane)):
                    side[k & 1, pl.ds(begin + i, GROUP, stride=span), :] = piece

    @pl.loop(0, count)
    def _(c):
        here = pl.ds(pl.multiple_of(c * span, GROUP), span)
        a = jnp.concatenate([left[0, here, :], left[1, here, :]], axis=1).astype(BF16)
        b = jnp.concatenate([right[0, here, :], right[1, here, :]], axis=1).astype(BF16)
        product = lax.dot_general(a, b, (((0,), (0,)), ((), ())), preferred_element_type=F32)
        there = pl.ds(pl.multiple_of(c * tall, GROUP), tall)
        total[0, there, :] = product[:, :LANES]
        total[1, there, :] = product[:, LANES:]

    @pl.loop(0, rows // GROUP)
    def _(step):
        lanes = pl.ds(pl.multiple_of(step * GROUP * width, LANES), GROUP * width)
        for k in range(8):
            target = dap ^ (k >> 1)
            begin = ((target >> 1) ^ sub) * LANES + (target & 1) * rows + step * GROUP
            pieces = [
                total[k & 1, pl.ds(begin + i, GROUP, stride=tall), :] for i in range(GROUP)
            ]
            outs[k][:, lanes] = join_group(pieces, width, lane).astype(BF16)


def output_weights(table, square, gain, meta, count):
    core, chip = meta[0], meta[1]
    mine = table.shape[0] // 2
    size = mine // count
    starts = [
        side * mine + size * ((chip & (count - 1)) ^ k)
        for side in (core, 1 - core)
        for k in range(count)
    ]
    square[...] = jnp.broadcast_to(gain, square.shape).T
    return pick_rows(table, starts, size).T.astype(BF16), pick_rows(square, starts, size)


def add_update(own, other, stream, gate, weights, factor, lanes):
    mixed = jnp.concatenate([own[:, lanes].astype(F32), other[:, lanes].astype(F32)], axis=0)
    middle = norm_rows(mixed, factor).astype(BF16)
    return stream[:, lanes] + gate[:, lanes] * jnp.dot(weights, middle, preferred_element_type=F32)


def second_kernel(
    meta, own, other, stream, gate, mask, entry_gain, weight, middle_gain, out_weight, *refs, width
):
    stream_out, normed_out, *messages, table, out_table, square = refs
    out_table[...] = out_weight[0].astype(F32)
    out_weights, middle = output_weights(out_table, square, middle_gain[0:1, :], meta, 4)
    table[...] = weight[1].astype(F32).T
    weights = side_weights(table, meta, True)
    middle_factor = jnp.concatenate([middle] * (width // middle.shape[1]), axis=1)
    factor = column_of(entry_gain[1:2, :], width)

    @pl.loop(0, stream.shape[1] // width)
    def _(step):
        lanes = pl.ds(pl.multiple_of(step * width, LANES), width)
        values = add_update(own, other, stream, gate, out_weights, middle_factor, lanes)
        stream_out[:, lanes] = values
        normed = norm_rows(values, factor).astype(BF16)
        normed_out[:, lanes] = normed
        send_sides(normed, weights, mask[:, lanes], messages, lanes, True)


def last_kernel(
    meta, own, other, stream, gate, middle_gain, out_weight, final_gain, expand, shrink, *refs, width
):
    result, out_table, square, both = refs
    core = meta[0]
    rows, cols, channels = result.shape
    out_table[...] = out_weight[1].astype(F32)
    out_weights, middle = output_weights(out_table, square, middle_gain[1:2, :], meta, 8)
    middle_factor = jnp.concatenate([middle] * (width // middle.shape[1]), axis=1)

    @pl.loop(0, rows // GROUP)
    def _(step):
        lanes = pl.ds(pl.multiple_of(step * width, LANES), width)
        values = add_update(own, other, stream, gate, out_weights, middle_factor, lanes)
        both[...] = values.T.reshape(GROUP, 2 * cols, channels)
        flat = both[:, pl.ds(pl.multiple_of(core * cols, GROUP), cols), :]
        flat = flat.reshape(GROUP * cols, channels)
        normed = layer_norm(flat, final_gain[...], 1).astype(BF16)
        expanded = jnp.dot(normed, expand[...], preferred_element_type=F32)
        expanded = jnp.maximum(expanded, 0.0).astype(BF16)
        out = flat + jnp.dot(expanded, shrink[...], preferred_element_type=F32)
        result[pl.ds(step * GROUP, GROUP)] = out.astype(BF16).reshape(GROUP, cols, channels)


def call(kernel, outs, scratch, args, scalars=1, flops=0):
    in_specs = [pl.BlockSpec(memory_space=pltpu.SMEM)] * scalars
    in_specs += [pl.BlockSpec(memory_space=pltpu.VMEM)] * (len(args) - scalars)
    moved = sum(a.size * a.dtype.itemsize for a in (*args, *outs))
    return pl.pallas_call(
        kernel,
        out_shape=outs,
        in_specs=in_specs,
        out_specs=[pl.BlockSpec(memory_space=pltpu.VMEM)] * len(outs),
        scratch_shapes=scratch,
        compiler_params=pltpu.CompilerParams(vmem_limit_bytes=40 * 1024 * 1024),
        cost_estimate=pl.CostEstimate(flops=flops, bytes_accessed=moved, transcendentals=0),
    )(*args)


def to_chip(value, distance):
    if distance == 0:
        return value
    pairs = [(device, device ^ (2 * distance)) for device in range(16)]
    return lax.ppermute(value, CHIPS, pairs)


def swap_cores(value):
    return lax.ppermute(value, "pair", [(0, 1), (1, 0)])


FAR_FIRST = (4, 5, 6, 7, 2, 3, 1, 0)


def chip_device(
    pair_input,
    residue_mask,
    entry_gain,
    input_weight,
    middle_gain,
    output_weight,
    final_gain,
    expand_weight,
    shrink_weight,
):
    rows, cols, channels = pair_input.shape
    hidden = output_weight.shape[1]
    width = 2 * cols
    pairs = rows * width
    wide = GROUP * width
    dap, sub, core = lax.axis_index("dap"), lax.axis_index("sub"), lax.axis_index("pair")
    meta = jnp.stack([core, dap * 2 + sub]).astype(jnp.int32)
    other_input = swap_cores(pair_input)
    mask_values = residue_mask.astype(F32)
    row_mask = lax.dynamic_slice_in_dim(mask_values, dap * rows, rows)
    col_mask = lax.dynamic_slice_in_dim(mask_values, sub * width, width)
    mask = (row_mask[:, None] * col_mask[None, :]).reshape(1, pairs)
    shape = jax.ShapeDtypeStruct
    flat32, flat16 = shape((channels, pairs), F32), shape((channels, pairs), BF16)
    quarter, eighth = hidden // 8, hidden // 16

    stream, normed, *messages = call(
        first_kernel,
        [flat32, flat16] + [shape((2 * quarter, pairs), BF16)] * 4 + [shape((quarter, pairs), BF16)] * 4,
        [pltpu.VMEM((rows, width, channels), F32), pltpu.VMEM((5 * hidden, channels), F32)],
        (meta, pair_input, other_input, mask, entry_gain, input_weight),
    )
    arrived = {k: to_chip(messages[k], k) for k in FAR_FIRST}
    (gate,) = call(
        functools.partial(gate_kernel, update=0), [flat32], [], (normed, input_weight), 0
    )
    sums = call(
        functools.partial(outgoing_kernel, rows=rows, width=width),
        [shape((quarter, pairs), BF16)] * 4,
        [
            pltpu.VMEM((2, quarter * 2 * rows, LANES), F32),
            pltpu.VMEM((2, quarter * 4 * rows, LANES), F32),
            pltpu.VMEM((2, quarter * 2 * rows, LANES), F32),
        ],
        (meta, *[arrived[k] for k in range(8)]),
    )
    returned = {k: to_chip(sums[k], k) for k in (2, 3, 1, 0)}
    own = jnp.concatenate([returned[k] for k in range(4)], axis=0)
    other = swap_cores(own)
    stream, normed, *messages = call(
        functools.partial(second_kernel, width=wide),
        [flat32, flat16] + [shape((2 * eighth, pairs), BF16)] * 8,
        [
            pltpu.VMEM((5 * hidden, channels), F32),
            pltpu.VMEM((hidden, channels), F32),
            pltpu.VMEM((hidden, LANES), F32),
        ],
        (meta, own, other, stream, gate, mask, entry_gain, input_weight, middle_gain, output_weight),
    )
    arrived = {k: to_chip(messages[k], k) for k in FAR_FIRST}
    (gate,) = call(
        functools.partial(gate_kernel, update=1), [flat32], [], (normed, input_weight), 0
    )
    sums = call(
        functools.partial(incoming_kernel, rows=rows, width=width),
        [shape((eighth, pairs), BF16)] * 8,
        [
            pltpu.VMEM((2, eighth * 4 * rows, LANES), F32),
            pltpu.VMEM((2, eighth * 4 * rows, LANES), F32),
            pltpu.VMEM((2, eighth * 2 * LANES, LANES), F32),
        ],
        (meta, *[arrived[k] for k in range(8)]),
    )
    returned = {k: to_chip(sums[k], k) for k in FAR_FIRST}
    own = jnp.concatenate([returned[k] for k in range(8)], axis=0)
    other = swap_cores(own)
    (result,) = call(
        functools.partial(last_kernel, width=wide),
        [shape((rows, cols, channels), BF16)],
        [
            pltpu.VMEM((hidden, channels), F32),
            pltpu.VMEM((hidden, LANES), F32),
            pltpu.VMEM((GROUP, width, channels), F32),
        ],
        (
            meta, own, other, stream, gate, middle_gain, output_weight,
            final_gain.reshape(1, channels), expand_weight, shrink_weight,
        ),
    )
    return result


def by_chips(mesh, pair_input, output_weight):
    sizes = dict(mesh.shape)
    rows = pair_input.shape[0] // (sizes["grp"] * sizes["dap"])
    cols = pair_input.shape[1] // (sizes["sub"] * sizes["pair"])
    return (
        (sizes["dap"], sizes["sub"], sizes["pair"]) == (4, 2, 2)
        and pair_input.shape[2] == LANES
        and output_weight.shape[1] == LANES
        and rows == cols
        and rows % GROUP == 0
        and 2 * cols <= LANES
        and GROUP * 2 * cols % LANES == 0
    )


def solution(mesh):
    placed = (P(("grp", "dap"), ("sub", "pair"), None), P("grp"), P(), P(), P(), P(), P(), P(), P())

    def run(*args):
        fits = by_chips(mesh, args[0], args[5])
        return jax.shard_map(
            chip_device if fits else general_device,
            mesh=mesh,
            in_specs=placed,
            out_specs=P(("grp", "dap"), ("sub", "pair"), None),
            check_vma=False,
        )(*args)

    return run
```

```python
import functools

import jax
import jax.numpy as jnp
from jax import lax
from jax.experimental import pallas as pl
from jax.experimental.pallas import tpu as pltpu
from jax.sharding import PartitionSpec as P

F32 = jnp.float32
BF16 = jnp.bfloat16
LANES = 128
GROUP = 8
CHIPS = ("dap", "sub", "pair")


def layer_norm(values, factor, dimension):
    average = jnp.mean(values, axis=dimension, keepdims=True)
    centred = values - average
    variance = jnp.mean(centred * centred, axis=dimension, keepdims=True)
    return centred * lax.rsqrt(variance + 1e-05) * factor


def spread_rows(left_side, right_side):
    return (
        lax.all_to_all(left_side, ("sub", "pair"), split_axis=0, concat_axis=2, tiled=True),
        lax.all_to_all(right_side, ("sub", "pair"), split_axis=0, concat_axis=2, tiled=True),
    )


def return_rows(mixed_sum):
    return lax.all_to_all(mixed_sum, ("sub", "pair"), split_axis=2, concat_axis=0, tiled=True)


def outgoing_rows(left_side, right_side):
    left_wide, right_wide = spread_rows(left_side, right_side)
    summed = jnp.einsum(
        "cik,cjk->cij",
        left_wide,
        lax.all_gather(right_wide, "dap", axis=1, tiled=True),
        preferred_element_type=jnp.float32,
    )
    return return_rows(summed.astype(jnp.bfloat16))


def incoming_rows(left_side, right_side):
    left_wide, right_wide = spread_rows(left_side, right_side)
    flipped = lax.all_to_all(left_wide, "dap", split_axis=2, concat_axis=1, tiled=True)
    summed = jnp.einsum(
        "cki,ckj->cij",
        flipped,
        lax.all_gather(right_wide, "dap", axis=1, tiled=True),
        preferred_element_type=jnp.float32,
    )
    return return_rows(summed.astype(jnp.bfloat16))


def triangle_update(
    stream, pair_mask, entry_gain, input_weight, middle_gain, output_weight, incoming
):
    row_count, col_count, channels = stream.shape
    hidden = output_weight.shape[0]
    normed = (
        layer_norm(stream, entry_gain, 2)
        .astype(jnp.bfloat16)
        .reshape(row_count * col_count, channels)
    )
    projected = lax.dot_general(
        input_weight[:, : 4 * hidden],
        normed,
        (((0,), (1,)), ((), ())),
        preferred_element_type=jnp.float32,
    )
    projected = projected.reshape(4 * hidden, row_count, col_count)
    left_side = (
        pair_mask * jax.nn.sigmoid(projected[hidden : 2 * hidden]) * projected[:hidden]
    ).astype(jnp.bfloat16)
    right_side = (
        pair_mask * jax.nn.sigmoid(projected[3 * hidden :]) * projected[2 * hidden : 3 * hidden]
    ).astype(jnp.bfloat16)
    gate_vals = jax.nn.sigmoid(
        jnp.dot(normed, input_weight[:, 4 * hidden :], preferred_element_type=jnp.float32)
    )
    mixed_sum = (
        incoming_rows(left_side, right_side) if incoming else outgoing_rows(left_side, right_side)
    )
    middle = layer_norm(mixed_sum.astype(jnp.float32), middle_gain[:, None, None], 0).astype(
        jnp.bfloat16
    )
    middle = middle.reshape(hidden, row_count * col_count)
    output = lax.dot_general(
        middle, output_weight, (((0,), (0,)), ((), ())), preferred_element_type=jnp.float32
    )
    return stream + (gate_vals * output).reshape(row_count, col_count, channels)


def general_device(
    pair_input,
    residue_mask,
    entry_gain,
    input_weight,
    middle_gain,
    output_weight,
    final_gain,
    expand_weight,
    shrink_weight,
):
    row_count, col_count, channels = pair_input.shape
    row_offset = lax.axis_index("dap") * row_count
    col_offset = lax.axis_index(("sub", "pair")) * col_count
    row_mask = lax.dynamic_slice_in_dim(residue_mask, row_offset, row_count).astype(jnp.float32)
    col_mask = lax.dynamic_slice_in_dim(residue_mask, col_offset, col_count).astype(jnp.float32)
    pair_mask = row_mask[:, None] * col_mask[None, :]
    stream = pair_input.astype(jnp.float32)
    for update_id in range(2):
        stream = triangle_update(
            stream,
            pair_mask,
            entry_gain[update_id],
            input_weight[update_id],
            middle_gain[update_id],
            output_weight[update_id],
            update_id == 1,
        )
    flat = stream.reshape(row_count * col_count, channels)
    normed = layer_norm(flat, final_gain, 1).astype(jnp.bfloat16)
    expanded = jax.nn.relu(
        jnp.dot(normed, expand_weight, preferred_element_type=jnp.float32)
    ).astype(jnp.bfloat16)
    result = flat + jnp.dot(expanded, shrink_weight, preferred_element_type=jnp.float32)
    return result.astype(jnp.bfloat16).reshape(row_count, col_count, channels)


def aligned(start, size):
    return start if isinstance(start, int) else pl.multiple_of(start, size)


def steps(count):
    def run(body):
        for step in range(count):
            body(step)

    return run


def sigmoid(values):
    return 0.5 * jnp.tanh(0.5 * values) + 0.5


def norm_rows(values, factor):
    average = jnp.mean(values, axis=0, keepdims=True)
    centred = values - average
    variance = jnp.mean(centred * centred, axis=0, keepdims=True)
    return centred * lax.rsqrt(variance + 1e-05) * factor


def column_of(gain_row, width):
    square = jnp.broadcast_to(gain_row, (gain_row.shape[1], gain_row.shape[1])).T
    return jnp.concatenate([square] * (width // square.shape[1]), axis=1)


def lane_index():
    return lax.broadcasted_iota(jnp.int32, (GROUP, LANES), 1)


def split_group(chunk, width, lane):
    pieces = []
    for row in range(GROUP):
        first, offset = divmod(row * width, LANES)
        piece = chunk[:, first * LANES : (first + 1) * LANES]
        if offset:
            piece = pltpu.roll(piece, LANES - offset, 1)
            if offset + width > LANES:
                after = chunk[:, (first + 1) * LANES : (first + 2) * LANES]
                after = pltpu.roll(after, LANES - offset, 1)
                piece = jnp.where(lane < LANES - offset, piece, after)
        pieces.append(jnp.where(lane < width, piece, 0.0))
    return pieces


def join_group(pieces, width, lane):
    parts = []
    for part in range(GROUP * width // LANES):
        begin = part * LANES
        value = None
        for row in range(begin // width, (begin + LANES - 1) // width + 1):
            shift = row * width - begin
            piece = pieces[row]
            if shift % LANES:
                piece = pltpu.roll(piece, shift % LANES, 1)
            value = piece if value is None else jnp.where(lane >= shift, piece, value)
        parts.append(value)
    return jnp.concatenate(parts, axis=1)


def pick_rows(table, starts, size):
    return jnp.concatenate(
        [table[pl.ds(aligned(start, GROUP), size), :] for start in starts], axis=0
    )


def side_weights(table, meta, incoming):
    core, chip = meta[0], meta[1]
    hidden = table.shape[0] // 5
    mine = hidden // 2
    count = 8 if incoming else 4
    size = mine // count
    picked = []
    for base in range(4):
        starts = [
            base * hidden + core * mine + size * ((chip & (count - 1)) ^ k) for k in range(count)
        ]
        picked.append(pick_rows(table, starts, size))
    return jnp.concatenate(picked, axis=0).astype(BF16)


def send_sides(normed, weights, mask, messages, lanes, incoming):
    quarter = weights.shape[0] // 4
    projected = jnp.dot(weights, normed, preferred_element_type=F32)
    left = mask * sigmoid(projected[quarter : 2 * quarter]) * projected[:quarter]
    right = mask * sigmoid(projected[3 * quarter :]) * projected[2 * quarter : 3 * quarter]
    count = 8 if incoming else 4
    size = quarter // count
    for k in range(count):
        rows = slice(k * size, (k + 1) * size)
        messages[k][:, lanes] = jnp.concatenate([left[rows], right[rows]], axis=0).astype(BF16)
        if not incoming:
            messages[4 + k][:, lanes] = right[rows].astype(BF16)


def first_kernel(meta, own, other, mask, gain, weight, *refs):
    stream, normed_out, *messages, both, table = refs
    core = meta[0]
    rows, cols, channels = own.shape
    both[:, pl.ds(aligned(core * cols, GROUP), cols), :] = own[...].astype(F32)
    both[:, pl.ds(aligned((1 - core) * cols, GROUP), cols), :] = other[...].astype(F32)
    table[...] = weight[0].astype(F32).T
    weights = side_weights(table, meta, False)
    width = GROUP * 2 * cols
    factor = column_of(gain[0:1, :], width)

    @steps(rows // GROUP)
    def _(step):
        lanes = pl.ds(aligned(step * width, LANES), width)
        values = both[pl.ds(step * GROUP, GROUP)].reshape(width, channels).T
        stream[:, lanes] = values
        normed = norm_rows(values, factor).astype(BF16)
        normed_out[:, lanes] = normed
        send_sides(normed, weights, mask[:, lanes], messages, lanes, False)


def gate_kernel(normed, weight, gate, *, update):
    channels = normed.shape[0]
    hidden = (weight.shape[2] - channels) // 4
    table = weight[update, :, 4 * hidden :].astype(F32).T.astype(BF16)
    gate[...] = sigmoid(jnp.dot(table, normed[...], preferred_element_type=F32))


def outgoing_kernel(meta, *refs, rows, width):
    messages, outs = dict(zip(SIDES_OUT, refs[:8])), refs[8:12]
    left, right, total = refs[12:]
    dap, sub = meta[1] >> 1, meta[1] & 1
    lane = lane_index()
    count = outs[0].shape[0]
    span = 2 * rows

    @steps(rows // GROUP)
    def _(step):
        lanes = pl.ds(aligned(step * GROUP * width, LANES), GROUP * width)
        for k in range(8):
            values = messages[k][:, lanes].astype(F32)
            source = dap ^ (k >> 1)
            half = (source >> 1) ^ sub
            near = (source & 1) * rows
            if k < 4:
                begin = ((k >> 1) & 1) * rows + step * GROUP
                for c in range(0, count, GROUP):
                    for i, piece in enumerate(split_group(values[c : c + GROUP], width, lane)):
                        left[k & 1, pl.ds(c * span + begin + i, GROUP, stride=span), :] = piece
                values = values[count:]
            begin = half * (count * span) + near + step * GROUP
            for c in range(0, count, GROUP):
                for i, piece in enumerate(split_group(values[c : c + GROUP], width, lane)):
                    right[k & 1, pl.ds(c * span + begin + i, GROUP, stride=span), :] = piece

    @steps(count)
    def _(c):
        here = pl.ds(aligned(c * span, GROUP), span)
        a = jnp.concatenate([left[0, here, :], left[1, here, :]], axis=1).astype(BF16)
        for half in range(2):
            there = pl.ds(aligned(half * (count * span) + c * span, GROUP), span)
            b = jnp.concatenate([right[0, there, :], right[1, there, :]], axis=1).astype(BF16)
            total[half, here, 0:width] = lax.dot_general(
                a, b, (((1,), (1,)), ((), ())), preferred_element_type=F32
            )

    @steps(rows // GROUP)
    def _(step):
        lanes = pl.ds(aligned(step * GROUP * width, LANES), GROUP * width)
        for k in range(4):
            begin = (k >> 1) * rows + step * GROUP
            joined = []
            for c in range(0, count, GROUP):
                pieces = [
                    total[k & 1, pl.ds(c * span + begin + i, GROUP, stride=span), :]
                    for i in range(GROUP)
                ]
                joined.append(join_group(pieces, width, lane))
            outs[k][:, lanes] = jnp.concatenate(joined, axis=0).astype(BF16)


def incoming_kernel(meta, *refs, rows, width):
    messages, outs = dict(zip(SIDES_IN, refs[:8])), refs[8:16]
    left, right, total = refs[16:]
    dap, sub = meta[1] >> 1, meta[1] & 1
    lane = lane_index()
    count = outs[0].shape[0]
    span = 4 * rows
    tall = 2 * LANES

    @steps(rows // GROUP)
    def _(step):
        lanes = pl.ds(aligned(step * GROUP * width, LANES), GROUP * width)
        for k in range(8):
            values = messages[k][:, lanes].astype(F32)
            begin = (k >> 1) * rows + step * GROUP
            for side, part in ((left, values[:count]), (right, values[count:])):
                for i, piece in enumerate(split_group(part, width, lane)):
                    side[k & 1, pl.ds(begin + i, GROUP, stride=span), :] = piece

    @steps(count)
    def _(c):
        here = pl.ds(aligned(c * span, GROUP), span)
        a = jnp.concatenate([left[0, here, :], left[1, here, :]], axis=1).astype(BF16)
        b = jnp.concatenate([right[0, here, :], right[1, here, :]], axis=1).astype(BF16)
        product = lax.dot_general(a, b, (((0,), (0,)), ((), ())), preferred_element_type=F32)
        there = pl.ds(aligned(c * tall, GROUP), tall)
        total[0, there, :] = product[:, :LANES]
        total[1, there, :] = product[:, LANES:]

    @steps(rows // GROUP)
    def _(step):
        lanes = pl.ds(aligned(step * GROUP * width, LANES), GROUP * width)
        for k in range(8):
            target = dap ^ (k >> 1)
            begin = ((target >> 1) ^ sub) * LANES + (target & 1) * rows + step * GROUP
            pieces = [
                total[k & 1, pl.ds(begin + i, GROUP, stride=tall), :] for i in range(GROUP)
            ]
            outs[k][:, lanes] = join_group(pieces, width, lane).astype(BF16)


def output_weights(table, square, gain, meta, order):
    core, chip = meta[0], meta[1]
    mine = table.shape[0] // 2
    size = mine // len(order)
    starts = [
        side * mine + size * ((chip & (len(order) - 1)) ^ k)
        for side in (core, 1 - core)
        for k in order
    ]
    square[...] = jnp.broadcast_to(gain, square.shape).T
    return pick_rows(table, starts, size).T.astype(BF16), pick_rows(square, starts, size)


def add_update(own, other, stream, gate, weights, factor, lanes):
    mixed = jnp.concatenate([own[:, lanes].astype(F32), other[:, lanes].astype(F32)], axis=0)
    middle = norm_rows(mixed, factor).astype(BF16)
    return stream[:, lanes] + gate[:, lanes] * jnp.dot(weights, middle, preferred_element_type=F32)


def second_kernel(
    meta, own, other, stream, gate, mask, entry_gain, weight, middle_gain, out_weight, *refs, width
):
    stream_out, normed_out, *messages, table, out_table, square = refs
    out_table[...] = out_weight[0].astype(F32)
    out_weights, middle = output_weights(out_table, square, middle_gain[0:1, :], meta, SUMS_OUT)
    table[...] = weight[1].astype(F32).T
    weights = side_weights(table, meta, True)
    middle_factor = jnp.concatenate([middle] * (width // middle.shape[1]), axis=1)
    factor = column_of(entry_gain[1:2, :], width)

    @steps(stream.shape[1] // width)
    def _(step):
        lanes = pl.ds(aligned(step * width, LANES), width)
        values = add_update(own, other, stream, gate, out_weights, middle_factor, lanes)
        stream_out[:, lanes] = values
        normed = norm_rows(values, factor).astype(BF16)
        normed_out[:, lanes] = normed
        send_sides(normed, weights, mask[:, lanes], messages, lanes, True)


def last_kernel(
    meta, own, other, stream, gate, middle_gain, out_weight, final_gain, expand, shrink, *refs, width
):
    result, out_table, square, both = refs
    core = meta[0]
    rows, cols, channels = result.shape
    out_table[...] = out_weight[1].astype(F32)
    out_weights, middle = output_weights(out_table, square, middle_gain[1:2, :], meta, SUMS_IN)
    middle_factor = jnp.concatenate([middle] * (width // middle.shape[1]), axis=1)

    @steps(rows // GROUP)
    def _(step):
        lanes = pl.ds(aligned(step * width, LANES), width)
        values = add_update(own, other, stream, gate, out_weights, middle_factor, lanes)
        both[...] = values.T.reshape(GROUP, 2 * cols, channels)
        flat = both[:, pl.ds(aligned(core * cols, GROUP), cols), :]
        flat = flat.reshape(GROUP * cols, channels)
        normed = layer_norm(flat, final_gain[...], 1).astype(BF16)
        expanded = jnp.dot(normed, expand[...], preferred_element_type=F32)
        expanded = jnp.maximum(expanded, 0.0).astype(BF16)
        out = flat + jnp.dot(expanded, shrink[...], preferred_element_type=F32)
        result[pl.ds(step * GROUP, GROUP)] = out.astype(BF16).reshape(GROUP, cols, channels)


def call(kernel, outs, scratch, args, scalars=1, flops=0):
    in_specs = [pl.BlockSpec(memory_space=pltpu.SMEM)] * scalars
    in_specs += [pl.BlockSpec(memory_space=pltpu.VMEM)] * (len(args) - scalars)
    moved = sum(a.size * a.dtype.itemsize for a in (*args, *outs))
    return pl.pallas_call(
        kernel,
        out_shape=outs,
        in_specs=in_specs,
        out_specs=[pl.BlockSpec(memory_space=pltpu.VMEM)] * len(outs),
        scratch_shapes=scratch,
        compiler_params=pltpu.CompilerParams(vmem_limit_bytes=40 * 1024 * 1024),
        cost_estimate=pl.CostEstimate(flops=flops, bytes_accessed=moved, transcendentals=0),
    )(*args)


def to_chip(value, distance):
    if distance == 0:
        return value
    pairs = [(device, device ^ (2 * distance)) for device in range(16)]
    return lax.ppermute(value, CHIPS, pairs)


def swap_cores(value):
    return lax.ppermute(value, "pair", [(0, 1), (1, 0)])


SIDES_OUT = (4, 5, 2, 6, 3, 7, 1, 0)
SIDES_IN = (4, 2, 5, 3, 6, 1, 7, 0)
SUMS_OUT = (3, 2, 1, 0)
SUMS_IN = (4, 5, 6, 2, 7, 3, 1, 0)


def chip_device(
    pair_input,
    residue_mask,
    entry_gain,
    input_weight,
    middle_gain,
    output_weight,
    final_gain,
    expand_weight,
    shrink_weight,
):
    rows, cols, channels = pair_input.shape
    hidden = output_weight.shape[1]
    width = 2 * cols
    pairs = rows * width
    wide = GROUP * width
    dap, sub, core = lax.axis_index("dap"), lax.axis_index("sub"), lax.axis_index("pair")
    meta = jnp.stack([core, dap * 2 + sub]).astype(jnp.int32)
    other_input = swap_cores(pair_input)
    mask_values = residue_mask.astype(F32)
    row_mask = lax.dynamic_slice_in_dim(mask_values, dap * rows, rows)
    col_mask = lax.dynamic_slice_in_dim(mask_values, sub * width, width)
    mask = (row_mask[:, None] * col_mask[None, :]).reshape(1, pairs)
    shape = jax.ShapeDtypeStruct
    flat32, flat16 = shape((channels, pairs), F32), shape((channels, pairs), BF16)
    quarter, eighth = hidden // 8, hidden // 16

    stream, normed, *messages = call(
        first_kernel,
        [flat32, flat16] + [shape((2 * quarter, pairs), BF16)] * 4 + [shape((quarter, pairs), BF16)] * 4,
        [pltpu.VMEM((rows, width, channels), F32), pltpu.VMEM((5 * hidden, channels), F32)],
        (meta, pair_input, other_input, mask, entry_gain, input_weight),
    )
    arrived = [to_chip(messages[k], k) for k in SIDES_OUT]
    (gate,) = call(
        functools.partial(gate_kernel, update=0), [flat32], [], (normed, input_weight), 0
    )
    sums = call(
        functools.partial(outgoing_kernel, rows=rows, width=width),
        [shape((quarter, pairs), BF16)] * 4,
        [
            pltpu.VMEM((2, quarter * 2 * rows, LANES), F32),
            pltpu.VMEM((2, quarter * 4 * rows, LANES), F32),
            pltpu.VMEM((2, quarter * 2 * rows, LANES), F32),
        ],
        (meta, *arrived),
    )
    own = jnp.concatenate([to_chip(sums[k], k) for k in SUMS_OUT], axis=0)
    other = swap_cores(own)
    stream, normed, *messages = call(
        functools.partial(second_kernel, width=wide),
        [flat32, flat16] + [shape((2 * eighth, pairs), BF16)] * 8,
        [
            pltpu.VMEM((5 * hidden, channels), F32),
            pltpu.VMEM((hidden, channels), F32),
            pltpu.VMEM((hidden, LANES), F32),
        ],
        (meta, own, other, stream, gate, mask, entry_gain, input_weight, middle_gain, output_weight),
    )
    arrived = [to_chip(messages[k], k) for k in SIDES_IN]
    (gate,) = call(
        functools.partial(gate_kernel, update=1), [flat32], [], (normed, input_weight), 0
    )
    sums = call(
        functools.partial(incoming_kernel, rows=rows, width=width),
        [shape((eighth, pairs), BF16)] * 8,
        [
            pltpu.VMEM((2, eighth * 4 * rows, LANES), F32),
            pltpu.VMEM((2, eighth * 4 * rows, LANES), F32),
            pltpu.VMEM((2, eighth * 2 * LANES, LANES), F32),
        ],
        (meta, *arrived),
    )
    own = jnp.concatenate([to_chip(sums[k], k) for k in SUMS_IN], axis=0)
    other = swap_cores(own)
    (result,) = call(
        functools.partial(last_kernel, width=wide),
        [shape((rows, cols, channels), BF16)],
        [
            pltpu.VMEM((hidden, channels), F32),
            pltpu.VMEM((hidden, LANES), F32),
            pltpu.VMEM((GROUP, width, channels), F32),
        ],
        (
            meta, own, other, stream, gate, middle_gain, output_weight,
            final_gain.reshape(1, channels), expand_weight, shrink_weight,
        ),
    )
    return result


def by_chips(mesh, pair_input, output_weight):
    sizes = dict(mesh.shape)
    rows = pair_input.shape[0] // (sizes["grp"] * sizes["dap"])
    cols = pair_input.shape[1] // (sizes["sub"] * sizes["pair"])
    return (
        (sizes["dap"], sizes["sub"], sizes["pair"]) == (4, 2, 2)
        and pair_input.shape[2] == LANES
        and output_weight.shape[1] == LANES
        and rows == cols
        and rows % GROUP == 0
        and 2 * cols <= LANES
        and GROUP * 2 * cols % LANES == 0
    )


def solution(mesh):
    placed = (P(("grp", "dap"), ("sub", "pair"), None), P("grp"), P(), P(), P(), P(), P(), P(), P())

    def run(*args):
        fits = by_chips(mesh, args[0], args[5])
        return jax.shard_map(
            chip_device if fits else general_device,
            mesh=mesh,
            in_specs=placed,
            out_specs=P(("grp", "dap"), ("sub", "pair"), None),
            check_vma=False,
        )(*args)

    return run
```

```python
import functools

import jax
import jax.numpy as jnp
from jax import lax
from jax.experimental import pallas as pl
from jax.experimental.pallas import tpu as pltpu
from jax.sharding import PartitionSpec as P

F32 = jnp.float32
BF16 = jnp.bfloat16
LANES = 128
GROUP = 8
CHIPS = ("dap", "sub", "pair")


def layer_norm(values, factor, dimension):
    average = jnp.mean(values, axis=dimension, keepdims=True)
    centred = values - average
    variance = jnp.mean(centred * centred, axis=dimension, keepdims=True)
    return centred * lax.rsqrt(variance + 1e-05) * factor


def spread_rows(left_side, right_side):
    return (
        lax.all_to_all(left_side, ("sub", "pair"), split_axis=0, concat_axis=2, tiled=True),
        lax.all_to_all(right_side, ("sub", "pair"), split_axis=0, concat_axis=2, tiled=True),
    )


def return_rows(mixed_sum):
    return lax.all_to_all(mixed_sum, ("sub", "pair"), split_axis=2, concat_axis=0, tiled=True)


def outgoing_rows(left_side, right_side):
    left_wide, right_wide = spread_rows(left_side, right_side)
    summed = jnp.einsum(
        "cik,cjk->cij",
        left_wide,
        lax.all_gather(right_wide, "dap", axis=1, tiled=True),
        preferred_element_type=jnp.float32,
    )
    return return_rows(summed.astype(jnp.bfloat16))


def incoming_rows(left_side, right_side):
    left_wide, right_wide = spread_rows(left_side, right_side)
    flipped = lax.all_to_all(left_wide, "dap", split_axis=2, concat_axis=1, tiled=True)
    summed = jnp.einsum(
        "cki,ckj->cij",
        flipped,
        lax.all_gather(right_wide, "dap", axis=1, tiled=True),
        preferred_element_type=jnp.float32,
    )
    return return_rows(summed.astype(jnp.bfloat16))


def triangle_update(
    stream, pair_mask, entry_gain, input_weight, middle_gain, output_weight, incoming
):
    row_count, col_count, channels = stream.shape
    hidden = output_weight.shape[0]
    normed = (
        layer_norm(stream, entry_gain, 2)
        .astype(jnp.bfloat16)
        .reshape(row_count * col_count, channels)
    )
    projected = lax.dot_general(
        input_weight[:, : 4 * hidden],
        normed,
        (((0,), (1,)), ((), ())),
        preferred_element_type=jnp.float32,
    )
    projected = projected.reshape(4 * hidden, row_count, col_count)
    left_side = (
        pair_mask * jax.nn.sigmoid(projected[hidden : 2 * hidden]) * projected[:hidden]
    ).astype(jnp.bfloat16)
    right_side = (
        pair_mask * jax.nn.sigmoid(projected[3 * hidden :]) * projected[2 * hidden : 3 * hidden]
    ).astype(jnp.bfloat16)
    gate_vals = jax.nn.sigmoid(
        jnp.dot(normed, input_weight[:, 4 * hidden :], preferred_element_type=jnp.float32)
    )
    mixed_sum = (
        incoming_rows(left_side, right_side) if incoming else outgoing_rows(left_side, right_side)
    )
    middle = layer_norm(mixed_sum.astype(jnp.float32), middle_gain[:, None, None], 0).astype(
        jnp.bfloat16
    )
    middle = middle.reshape(hidden, row_count * col_count)
    output = lax.dot_general(
        middle, output_weight, (((0,), (0,)), ((), ())), preferred_element_type=jnp.float32
    )
    return stream + (gate_vals * output).reshape(row_count, col_count, channels)


def general_device(
    pair_input,
    residue_mask,
    entry_gain,
    input_weight,
    middle_gain,
    output_weight,
    final_gain,
    expand_weight,
    shrink_weight,
):
    row_count, col_count, channels = pair_input.shape
    row_offset = lax.axis_index("dap") * row_count
    col_offset = lax.axis_index(("sub", "pair")) * col_count
    row_mask = lax.dynamic_slice_in_dim(residue_mask, row_offset, row_count).astype(jnp.float32)
    col_mask = lax.dynamic_slice_in_dim(residue_mask, col_offset, col_count).astype(jnp.float32)
    pair_mask = row_mask[:, None] * col_mask[None, :]
    stream = pair_input.astype(jnp.float32)
    for update_id in range(2):
        stream = triangle_update(
            stream,
            pair_mask,
            entry_gain[update_id],
            input_weight[update_id],
            middle_gain[update_id],
            output_weight[update_id],
            update_id == 1,
        )
    flat = stream.reshape(row_count * col_count, channels)
    normed = layer_norm(flat, final_gain, 1).astype(jnp.bfloat16)
    expanded = jax.nn.relu(
        jnp.dot(normed, expand_weight, preferred_element_type=jnp.float32)
    ).astype(jnp.bfloat16)
    result = flat + jnp.dot(expanded, shrink_weight, preferred_element_type=jnp.float32)
    return result.astype(jnp.bfloat16).reshape(row_count, col_count, channels)


EVERYWHERE = (4, 5, 2, 6, 3, 7, 1, 0)
WITHIN_HALF = (3, 2, 1, 0)


def aligned(start, size):
    return start if isinstance(start, int) else pl.multiple_of(start, size)


def steps(count):
    def run(body):
        for step in range(count):
            body(step)

    return run


def sigmoid(values):
    return 0.5 * jnp.tanh(0.5 * values) + 0.5


def norm_rows(values, factor):
    average = jnp.mean(values, axis=0, keepdims=True)
    centred = values - average
    variance = jnp.mean(centred * centred, axis=0, keepdims=True)
    return centred * lax.rsqrt(variance + 1e-05) * factor


def column_of(gain_row, width):
    square = jnp.broadcast_to(gain_row, (gain_row.shape[1], gain_row.shape[1])).T
    return jnp.concatenate([square] * (width // square.shape[1]), axis=1)


def lane_index():
    return lax.broadcasted_iota(jnp.int32, (GROUP, LANES), 1)


def split_group(chunk, width, lane):
    pieces = []
    for row in range(GROUP):
        first, offset = divmod(row * width, LANES)
        piece = chunk[:, first * LANES : (first + 1) * LANES]
        if offset:
            piece = pltpu.roll(piece, LANES - offset, 1)
            if offset + width > LANES:
                after = chunk[:, (first + 1) * LANES : (first + 2) * LANES]
                after = pltpu.roll(after, LANES - offset, 1)
                piece = jnp.where(lane < LANES - offset, piece, after)
        pieces.append(jnp.where(lane < width, piece, 0.0))
    return pieces


def join_group(pieces, width, lane):
    parts = []
    for part in range(GROUP * width // LANES):
        begin = part * LANES
        value = None
        for row in range(begin // width, (begin + LANES - 1) // width + 1):
            shift = row * width - begin
            piece = pieces[row]
            if shift % LANES:
                piece = pltpu.roll(piece, shift % LANES, 1)
            value = piece if value is None else jnp.where(lane >= shift, piece, value)
        parts.append(value)
    return jnp.concatenate(parts, axis=1)


def pick_rows(table, starts, size):
    return jnp.concatenate(
        [table[pl.ds(aligned(start, GROUP), size), :] for start in starts], axis=0
    )


def side_weights(table, meta):
    core, chip = meta[0], meta[1]
    hidden = table.shape[0] // 5
    mine = hidden // 2
    size = mine // 4
    picked = []
    for base in range(4):
        starts = [base * hidden + core * mine + size * ((chip & 3) ^ k) for k in range(4)]
        picked.append(pick_rows(table, starts, size))
    return jnp.concatenate(picked, axis=0).astype(BF16)


def send_sides(normed, weights, mask, messages, lanes):
    quarter = weights.shape[0] // 4
    projected = jnp.dot(weights, normed, preferred_element_type=F32)
    left = mask * sigmoid(projected[quarter : 2 * quarter]) * projected[:quarter]
    right = mask * sigmoid(projected[3 * quarter :]) * projected[2 * quarter : 3 * quarter]
    size = quarter // 4
    for k in range(4):
        rows = slice(k * size, (k + 1) * size)
        messages[k][:, lanes] = jnp.concatenate([left[rows], right[rows]], axis=0).astype(BF16)
        if len(messages) > 4:
            messages[4 + k][:, lanes] = right[rows].astype(BF16)


def first_kernel(meta, own, other, mask, gain, weight, *refs):
    stream, normed_out, *messages, both, table = refs
    core = meta[0]
    rows, cols, channels = own.shape
    both[:, pl.ds(aligned(core * cols, GROUP), cols), :] = own[...].astype(F32)
    both[:, pl.ds(aligned((1 - core) * cols, GROUP), cols), :] = other[...].astype(F32)
    table[...] = weight[0].astype(F32).T
    weights = side_weights(table, meta)
    width = GROUP * 2 * cols
    factor = column_of(gain[0:1, :], width)

    @steps(rows // GROUP)
    def _(step):
        lanes = pl.ds(aligned(step * width, LANES), width)
        values = both[pl.ds(step * GROUP, GROUP)].reshape(width, channels).T
        stream[:, lanes] = values
        normed = norm_rows(values, factor).astype(BF16)
        normed_out[:, lanes] = normed
        send_sides(normed, weights, mask[:, lanes], messages, lanes)


def gate_kernel(normed, weight, gate, *, update):
    channels = normed.shape[0]
    hidden = (weight.shape[2] - channels) // 4
    table = weight[update, :, 4 * hidden :].astype(F32).T.astype(BF16)
    gate[...] = sigmoid(jnp.dot(table, normed[...], preferred_element_type=F32))


def outgoing_kernel(meta, *refs, rows, width):
    messages, outs = dict(zip(EVERYWHERE, refs[:8])), refs[8:12]
    left, right, total = refs[12:]
    dap, sub = meta[1] >> 1, meta[1] & 1
    lane = lane_index()
    count = outs[0].shape[0]
    span = 2 * rows
    pitch = span + GROUP

    @steps(rows // GROUP)
    def _(step):
        lanes = pl.ds(aligned(step * GROUP * width, LANES), GROUP * width)
        for k in range(8):
            values = messages[k][:, lanes].astype(F32)
            source = dap ^ (k >> 1)
            half = (source >> 1) ^ sub
            near = (source & 1) * rows
            if k < 4:
                begin = ((k >> 1) & 1) * rows + step * GROUP
                for c in range(0, count, GROUP):
                    for i, piece in enumerate(split_group(values[c : c + GROUP], width, lane)):
                        left[k & 1, pl.ds(c * pitch + begin + i, GROUP, stride=pitch), :] = piece
                values = values[count:]
            begin = half * (count * pitch) + near + step * GROUP
            for c in range(0, count, GROUP):
                for i, piece in enumerate(split_group(values[c : c + GROUP], width, lane)):
                    right[k & 1, pl.ds(c * pitch + begin + i, GROUP, stride=pitch), :] = piece

    @steps(count)
    def _(c):
        here = pl.ds(aligned(c * pitch, GROUP), span)
        a = jnp.concatenate([left[0, here, :], left[1, here, :]], axis=1).astype(BF16)
        for half in range(2):
            there = pl.ds(aligned(half * (count * pitch) + c * pitch, GROUP), span)
            b = jnp.concatenate([right[0, there, :], right[1, there, :]], axis=1).astype(BF16)
            total[half, here, 0:width] = lax.dot_general(
                a, b, (((1,), (1,)), ((), ())), preferred_element_type=F32
            )

    @steps(rows // GROUP)
    def _(step):
        lanes = pl.ds(aligned(step * GROUP * width, LANES), GROUP * width)
        for k in range(4):
            begin = (k >> 1) * rows + step * GROUP
            joined = []
            for c in range(0, count, GROUP):
                pieces = [
                    total[k & 1, pl.ds(c * pitch + begin + i, GROUP, stride=pitch), :]
                    for i in range(GROUP)
                ]
                joined.append(join_group(pieces, width, lane))
            outs[k][:, lanes] = jnp.concatenate(joined, axis=0).astype(BF16)


def incoming_kernel(meta, *refs, rows, width):
    messages, outs = dict(zip(WITHIN_HALF, refs[:4])), refs[4:12]
    left, right, total = refs[12:]
    dap, sub = meta[1] >> 1, meta[1] & 1
    lane = lane_index()
    count = outs[0].shape[0]
    span = 2 * rows
    pitch = span + GROUP
    tall = 2 * width
    tall_pitch = tall + GROUP

    @steps(rows // GROUP)
    def _(step):
        lanes = pl.ds(aligned(step * GROUP * width, LANES), GROUP * width)
        for k in range(4):
            values = messages[k][:, lanes].astype(F32)
            begin = (k >> 1) * rows + step * GROUP
            for side, part in ((left, values[:count]), (right, values[count:])):
                for c in range(0, count, GROUP):
                    for i, piece in enumerate(split_group(part[c : c + GROUP], width, lane)):
                        side[k & 1, pl.ds(c * pitch + begin + i, GROUP, stride=pitch), :] = piece

    @steps(count)
    def _(c):
        here = pl.ds(aligned(c * pitch, GROUP), span)
        b = jnp.concatenate([right[0, here, :], right[1, here, :]], axis=1).astype(BF16)
        for block in range(2):
            a = left[block, here, 0:width].astype(BF16)
            product = lax.dot_general(a, b, (((0,), (0,)), ((), ())), preferred_element_type=F32)
            there = pl.ds(aligned(c * tall_pitch + block * width, GROUP), width)
            total[0, there, :] = product[:, :LANES]
            total[1, there, :] = product[:, LANES:]

    @steps(rows // GROUP)
    def _(step):
        lanes = pl.ds(aligned(step * GROUP * width, LANES), GROUP * width)
        for k in range(8):
            target = dap ^ (k >> 1)
            begin = ((target >> 1) ^ sub) * width + (target & 1) * rows + step * GROUP
            joined = []
            for c in range(0, count, GROUP):
                pieces = [
                    total[k & 1, pl.ds(c * tall_pitch + begin + i, GROUP, stride=tall_pitch), :]
                    for i in range(GROUP)
                ]
                joined.append(join_group(pieces, width, lane))
            outs[k][:, lanes] = jnp.concatenate(joined, axis=0).astype(BF16)


def output_weights(table, square, gain, meta):
    core, chip = meta[0], meta[1]
    mine = table.shape[0] // 2
    size = mine // 4
    starts = [
        side * mine + size * ((chip & 3) ^ k) for side in (core, 1 - core) for k in range(4)
    ]
    square[...] = jnp.broadcast_to(gain, square.shape).T
    return pick_rows(table, starts, size).T.astype(BF16), pick_rows(square, starts, size)


def add_update(own, other, stream, gate, weights, factor, lanes):
    mixed = jnp.concatenate([own[:, lanes].astype(F32), other[:, lanes].astype(F32)], axis=0)
    middle = norm_rows(mixed, factor).astype(BF16)
    return stream[:, lanes] + gate[:, lanes] * jnp.dot(weights, middle, preferred_element_type=F32)


def second_kernel(
    meta, own, other, stream, gate, mask, entry_gain, weight, middle_gain, out_weight, *refs, width
):
    stream_out, normed_out, *messages, table, out_table, square = refs
    out_table[...] = out_weight[0].astype(F32)
    out_weights, middle = output_weights(out_table, square, middle_gain[0:1, :], meta)
    table[...] = weight[1].astype(F32).T
    weights = side_weights(table, meta)
    middle_factor = jnp.concatenate([middle] * (width // middle.shape[1]), axis=1)
    factor = column_of(entry_gain[1:2, :], width)

    @steps(stream.shape[1] // width)
    def _(step):
        lanes = pl.ds(aligned(step * width, LANES), width)
        values = add_update(own, other, stream, gate, out_weights, middle_factor, lanes)
        stream_out[:, lanes] = values
        normed = norm_rows(values, factor).astype(BF16)
        normed_out[:, lanes] = normed
        send_sides(normed, weights, mask[:, lanes], messages, lanes)


def last_kernel(
    meta, own, other, stream, gate, middle_gain, out_weight, final_gain, expand, shrink, *refs, width
):
    result, out_table, square, both = refs
    core = meta[0]
    rows, cols, channels = result.shape
    out_table[...] = out_weight[1].astype(F32)
    out_weights, middle = output_weights(out_table, square, middle_gain[1:2, :], meta)
    middle_factor = jnp.concatenate([middle] * (width // middle.shape[1]), axis=1)

    @steps(rows // GROUP)
    def _(step):
        lanes = pl.ds(aligned(step * width, LANES), width)
        values = add_update(own, other, stream, gate, out_weights, middle_factor, lanes)
        both[...] = values.T.reshape(GROUP, 2 * cols, channels)
        flat = both[:, pl.ds(aligned(core * cols, GROUP), cols), :]
        flat = flat.reshape(GROUP * cols, channels)
        normed = layer_norm(flat, final_gain[...], 1).astype(BF16)
        expanded = jnp.dot(normed, expand[...], preferred_element_type=F32)
        expanded = jnp.maximum(expanded, 0.0).astype(BF16)
        out = flat + jnp.dot(expanded, shrink[...], preferred_element_type=F32)
        result[pl.ds(step * GROUP, GROUP)] = out.astype(BF16).reshape(GROUP, cols, channels)


def call(kernel, outs, scratch, args, scalars=1, flops=0):
    in_specs = [pl.BlockSpec(memory_space=pltpu.SMEM)] * scalars
    in_specs += [pl.BlockSpec(memory_space=pltpu.VMEM)] * (len(args) - scalars)
    moved = sum(a.size * a.dtype.itemsize for a in (*args, *outs))
    return pl.pallas_call(
        kernel,
        out_shape=outs,
        in_specs=in_specs,
        out_specs=[pl.BlockSpec(memory_space=pltpu.VMEM)] * len(outs),
        scratch_shapes=scratch,
        compiler_params=pltpu.CompilerParams(vmem_limit_bytes=40 * 1024 * 1024),
        cost_estimate=pl.CostEstimate(flops=flops, bytes_accessed=moved, transcendentals=0),
    )(*args)


def to_chip(value, distance):
    if distance == 0:
        return value
    pairs = [(device, device ^ (2 * distance)) for device in range(16)]
    return lax.ppermute(value, CHIPS, pairs)


def swap_cores(value):
    return lax.ppermute(value, "pair", [(0, 1), (1, 0)])


def chip_device(
    pair_input,
    residue_mask,
    entry_gain,
    input_weight,
    middle_gain,
    output_weight,
    final_gain,
    expand_weight,
    shrink_weight,
):
    rows, cols, channels = pair_input.shape
    hidden = output_weight.shape[1]
    width = 2 * cols
    pairs = rows * width
    wide = GROUP * width
    dap, sub, core = lax.axis_index("dap"), lax.axis_index("sub"), lax.axis_index("pair")
    meta = jnp.stack([core, dap * 2 + sub]).astype(jnp.int32)
    other_input = swap_cores(pair_input)
    mask_values = residue_mask.astype(F32)
    row_mask = lax.dynamic_slice_in_dim(mask_values, dap * rows, rows)
    col_mask = lax.dynamic_slice_in_dim(mask_values, sub * width, width)
    mask = (row_mask[:, None] * col_mask[None, :]).reshape(1, pairs)
    shape = jax.ShapeDtypeStruct
    flat32, flat16 = shape((channels, pairs), F32), shape((channels, pairs), BF16)
    part = hidden // 8
    sides, rights = shape((2 * part, pairs), BF16), shape((part, pairs), BF16)
    span, tall = 2 * rows + GROUP, 2 * width + GROUP

    stream, normed, *messages = call(
        first_kernel,
        [flat32, flat16] + [sides] * 4 + [rights] * 4,
        [pltpu.VMEM((rows, width, channels), F32), pltpu.VMEM((5 * hidden, channels), F32)],
        (meta, pair_input, other_input, mask, entry_gain, input_weight),
    )
    arrived = [to_chip(messages[k], k) for k in EVERYWHERE]
    (gate,) = call(
        functools.partial(gate_kernel, update=0), [flat32], [], (normed, input_weight), 0
    )
    sums = call(
        functools.partial(outgoing_kernel, rows=rows, width=width),
        [rights] * 4,
        [
            pltpu.VMEM((2, part * span, LANES), F32),
            pltpu.VMEM((2, 2 * part * span, LANES), F32),
            pltpu.VMEM((2, part * span, LANES), F32),
        ],
        (meta, *arrived),
    )
    returned = [to_chip(sums[k], k) for k in WITHIN_HALF]
    own = jnp.concatenate(returned[::-1], axis=0)
    other = swap_cores(own)
    stream, normed, *messages = call(
        functools.partial(second_kernel, width=wide),
        [flat32, flat16] + [sides] * 4,
        [
            pltpu.VMEM((5 * hidden, channels), F32),
            pltpu.VMEM((hidden, channels), F32),
            pltpu.VMEM((hidden, LANES), F32),
        ],
        (meta, own, other, stream, gate, mask, entry_gain, input_weight, middle_gain, output_weight),
    )
    arrived = [to_chip(messages[k], k) for k in WITHIN_HALF]
    (gate,) = call(
        functools.partial(gate_kernel, update=1), [flat32], [], (normed, input_weight), 0
    )
    sums = call(
        functools.partial(incoming_kernel, rows=rows, width=width),
        [rights] * 8,
        [
            pltpu.VMEM((2, part * span, LANES), F32),
            pltpu.VMEM((2, part * span, LANES), F32),
            pltpu.VMEM((2, part * tall, LANES), F32),
        ],
        (meta, *arrived),
    )
    returned = {k: to_chip(sums[k], k) for k in EVERYWHERE}
    near = jnp.concatenate([returned[k] for k in range(4)], axis=0)
    far = jnp.concatenate([returned[4 + k] for k in range(4)], axis=0)
    own = (near.astype(F32) + far.astype(F32)).astype(BF16)
    other = swap_cores(own)
    (result,) = call(
        functools.partial(last_kernel, width=wide),
        [shape((rows, cols, channels), BF16)],
        [
            pltpu.VMEM((hidden, channels), F32),
            pltpu.VMEM((hidden, LANES), F32),
            pltpu.VMEM((GROUP, width, channels), F32),
        ],
        (
            meta, own, other, stream, gate, middle_gain, output_weight,
            final_gain.reshape(1, channels), expand_weight, shrink_weight,
        ),
    )
    return result


def by_chips(mesh, pair_input, output_weight):
    sizes = dict(mesh.shape)
    rows = pair_input.shape[0] // (sizes["grp"] * sizes["dap"])
    cols = pair_input.shape[1] // (sizes["sub"] * sizes["pair"])
    return (
        (sizes["dap"], sizes["sub"], sizes["pair"]) == (4, 2, 2)
        and pair_input.shape[2] == LANES
        and output_weight.shape[1] == LANES
        and rows == cols
        and rows % GROUP == 0
        and 2 * cols <= LANES
        and GROUP * 2 * cols % LANES == 0
    )


def solution(mesh):
    placed = (P(("grp", "dap"), ("sub", "pair"), None), P("grp"), P(), P(), P(), P(), P(), P(), P())

    def run(*args):
        fits = by_chips(mesh, args[0], args[5])
        return jax.shard_map(
            chip_device if fits else general_device,
            mesh=mesh,
            in_specs=placed,
            out_specs=P(("grp", "dap"), ("sub", "pair"), None),
            check_vma=False,
        )(*args)

    return run
```

```python
import functools

import jax
import jax.numpy as jnp
from jax import lax
from jax.experimental import pallas as pl
from jax.experimental.pallas import tpu as pltpu
from jax.sharding import PartitionSpec as P

F32 = jnp.float32
BF16 = jnp.bfloat16
LANES = 128
GROUP = 8
CHIPS = ("dap", "sub", "pair")


def layer_norm(values, factor, dimension):
    average = jnp.mean(values, axis=dimension, keepdims=True)
    centred = values - average
    variance = jnp.mean(centred * centred, axis=dimension, keepdims=True)
    return centred * lax.rsqrt(variance + 1e-05) * factor


def spread_rows(left_side, right_side):
    return (
        lax.all_to_all(left_side, ("sub", "pair"), split_axis=0, concat_axis=2, tiled=True),
        lax.all_to_all(right_side, ("sub", "pair"), split_axis=0, concat_axis=2, tiled=True),
    )


def return_rows(mixed_sum):
    return lax.all_to_all(mixed_sum, ("sub", "pair"), split_axis=2, concat_axis=0, tiled=True)


def outgoing_rows(left_side, right_side):
    left_wide, right_wide = spread_rows(left_side, right_side)
    summed = jnp.einsum(
        "cik,cjk->cij",
        left_wide,
        lax.all_gather(right_wide, "dap", axis=1, tiled=True),
        preferred_element_type=jnp.float32,
    )
    return return_rows(summed.astype(jnp.bfloat16))


def incoming_rows(left_side, right_side):
    left_wide, right_wide = spread_rows(left_side, right_side)
    flipped = lax.all_to_all(left_wide, "dap", split_axis=2, concat_axis=1, tiled=True)
    summed = jnp.einsum(
        "cki,ckj->cij",
        flipped,
        lax.all_gather(right_wide, "dap", axis=1, tiled=True),
        preferred_element_type=jnp.float32,
    )
    return return_rows(summed.astype(jnp.bfloat16))


def triangle_update(
    stream, pair_mask, entry_gain, input_weight, middle_gain, output_weight, incoming
):
    row_count, col_count, channels = stream.shape
    hidden = output_weight.shape[0]
    normed = (
        layer_norm(stream, entry_gain, 2)
        .astype(jnp.bfloat16)
        .reshape(row_count * col_count, channels)
    )
    projected = lax.dot_general(
        input_weight[:, : 4 * hidden],
        normed,
        (((0,), (1,)), ((), ())),
        preferred_element_type=jnp.float32,
    )
    projected = projected.reshape(4 * hidden, row_count, col_count)
    left_side = (
        pair_mask * jax.nn.sigmoid(projected[hidden : 2 * hidden]) * projected[:hidden]
    ).astype(jnp.bfloat16)
    right_side = (
        pair_mask * jax.nn.sigmoid(projected[3 * hidden :]) * projected[2 * hidden : 3 * hidden]
    ).astype(jnp.bfloat16)
    gate_vals = jax.nn.sigmoid(
        jnp.dot(normed, input_weight[:, 4 * hidden :], preferred_element_type=jnp.float32)
    )
    mixed_sum = (
        incoming_rows(left_side, right_side) if incoming else outgoing_rows(left_side, right_side)
    )
    middle = layer_norm(mixed_sum.astype(jnp.float32), middle_gain[:, None, None], 0).astype(
        jnp.bfloat16
    )
    middle = middle.reshape(hidden, row_count * col_count)
    output = lax.dot_general(
        middle, output_weight, (((0,), (0,)), ((), ())), preferred_element_type=jnp.float32
    )
    return stream + (gate_vals * output).reshape(row_count, col_count, channels)


def general_device(
    pair_input,
    residue_mask,
    entry_gain,
    input_weight,
    middle_gain,
    output_weight,
    final_gain,
    expand_weight,
    shrink_weight,
):
    row_count, col_count, channels = pair_input.shape
    row_offset = lax.axis_index("dap") * row_count
    col_offset = lax.axis_index(("sub", "pair")) * col_count
    row_mask = lax.dynamic_slice_in_dim(residue_mask, row_offset, row_count).astype(jnp.float32)
    col_mask = lax.dynamic_slice_in_dim(residue_mask, col_offset, col_count).astype(jnp.float32)
    pair_mask = row_mask[:, None] * col_mask[None, :]
    stream = pair_input.astype(jnp.float32)
    for update_id in range(2):
        stream = triangle_update(
            stream,
            pair_mask,
            entry_gain[update_id],
            input_weight[update_id],
            middle_gain[update_id],
            output_weight[update_id],
            update_id == 1,
        )
    flat = stream.reshape(row_count * col_count, channels)
    normed = layer_norm(flat, final_gain, 1).astype(jnp.bfloat16)
    expanded = jax.nn.relu(
        jnp.dot(normed, expand_weight, preferred_element_type=jnp.float32)
    ).astype(jnp.bfloat16)
    result = flat + jnp.dot(expanded, shrink_weight, preferred_element_type=jnp.float32)
    return result.astype(jnp.bfloat16).reshape(row_count, col_count, channels)


EVERYWHERE = (4, 5, 2, 6, 3, 7, 1, 0)
WITHIN_HALF = (3, 2, 1, 0)


def aligned(start, size):
    return start if isinstance(start, int) else pl.multiple_of(start, size)


def steps(count):
    def run(body):
        for step in range(count):
            body(step)

    return run


def blocks(count, size=2 * LANES):
    def run(body):
        for begin in range(0, count, size):
            body(slice(begin, min(begin + size, count)))

    return run


def sigmoid(values):
    return 0.5 * jnp.tanh(0.5 * values) + 0.5


def norm_rows(values, factor):
    return jnp.concatenate(
        [
            norm_block(values[:, b : b + LANES], factor[:, :LANES])
            for b in range(0, values.shape[1], LANES)
        ],
        axis=1,
    )


def norm_block(values, factor):
    average = jnp.mean(values, axis=0, keepdims=True)
    centred = values - average
    variance = jnp.mean(centred * centred, axis=0, keepdims=True)
    return centred * lax.rsqrt(variance + 1e-05) * factor


def column_of(gain_row, width):
    square = jnp.broadcast_to(gain_row, (gain_row.shape[1], gain_row.shape[1])).T
    return jnp.concatenate([square] * (width // square.shape[1]), axis=1)


def lane_index():
    return lax.broadcasted_iota(jnp.int32, (GROUP, LANES), 1)


def split_group(chunk, width, lane):
    pieces = []
    for row in range(GROUP):
        first, offset = divmod(row * width, LANES)
        piece = chunk[:, first * LANES : (first + 1) * LANES]
        if offset:
            piece = pltpu.roll(piece, LANES - offset, 1)
            if offset + width > LANES:
                after = chunk[:, (first + 1) * LANES : (first + 2) * LANES]
                after = pltpu.roll(after, LANES - offset, 1)
                piece = jnp.where(lane < LANES - offset, piece, after)
        pieces.append(jnp.where(lane < width, piece, 0.0))
    return pieces


def join_group(pieces, width, lane):
    parts = []
    for part in range(GROUP * width // LANES):
        begin = part * LANES
        value = None
        for row in range(begin // width, (begin + LANES - 1) // width + 1):
            shift = row * width - begin
            piece = pieces[row]
            if shift % LANES:
                piece = pltpu.roll(piece, shift % LANES, 1)
            value = piece if value is None else jnp.where(lane >= shift, piece, value)
        parts.append(value)
    return jnp.concatenate(parts, axis=1)


def pick_rows(table, starts, size):
    return jnp.concatenate(
        [table[pl.ds(aligned(start, GROUP), size), :] for start in starts], axis=0
    )


def side_weights(table, meta):
    core, chip = meta[0], meta[1]
    hidden = table.shape[0] // 4
    mine = hidden // 2
    size = mine // 4
    picked = []
    for base in range(4):
        starts = [base * hidden + core * mine + size * ((chip & 3) ^ k) for k in range(4)]
        picked.append(pick_rows(table, starts, size))
    return jnp.concatenate(picked, axis=0).astype(BF16)


def send_sides(normed, weights, mask, messages, lanes):
    quarter = weights.shape[0] // 4
    projected = jnp.dot(weights, normed, preferred_element_type=F32)
    left = mask * sigmoid(projected[quarter : 2 * quarter]) * projected[:quarter]
    right = mask * sigmoid(projected[3 * quarter :]) * projected[2 * quarter : 3 * quarter]
    size = quarter // 4
    for k in range(4):
        rows = slice(k * size, (k + 1) * size)
        messages[k][:, lanes] = jnp.concatenate([left[rows], right[rows]], axis=0).astype(BF16)
        if len(messages) > 4:
            messages[4 + k][:, lanes] = right[rows].astype(BF16)


def pick_columns(first, own, other):
    return jnp.where(
        first, jnp.concatenate([own, other], axis=1), jnp.concatenate([other, own], axis=1)
    )


def first_kernel(meta, own, other, mask, weight, *refs):
    stream, normed_out, *messages, table = refs
    first = meta[0] == 0
    rows, cols, channels = own.shape
    width = GROUP * 2 * cols
    factors = column_of(mask[:, stream.shape[1] :], channels)
    table[...] = weight[...].astype(F32).T
    weights = side_weights(table, meta)

    @steps(rows // GROUP)
    def _(step):
        lanes = pl.ds(step * width, width)
        here = pl.ds(step * GROUP, GROUP)
        values = pick_columns(first, own[here].astype(F32), other[here].astype(F32))
        values = values.reshape(width, channels).T
        stream[:, lanes] = values

    @blocks(stream.shape[1])
    def _(lanes):
        normed = norm_rows(stream[:, lanes], factors).astype(BF16)
        normed_out[:, lanes] = normed
        send_sides(normed, weights, mask[:, lanes], messages, lanes)


def gate_of(normed, weight, update):
    channels = normed.shape[0]
    hidden = (weight.shape[2] - channels) // 4
    table = weight[update, :, 4 * hidden :].astype(F32).T.astype(BF16)
    return sigmoid(jnp.dot(table, normed[...], preferred_element_type=F32))


def first_gate_kernel(meta, normed, weight, entry_gain, middle_gain, out_weight, *refs):
    gate, out_weights, middle, factor, weights, table, out_table, square = refs
    gate[...] = gate_of(normed, weight, 0)
    out_table[...] = out_weight[0].astype(F32)
    out_weights[...], middle[...] = output_weights(out_table, square, middle_gain[0:1, :], meta)
    factor[...] = column_of(entry_gain[1:2, :], factor.shape[1])
    table[...] = weight[1, :, : table.shape[0]].astype(F32).T
    weights[...] = side_weights(table, meta)


def second_gate_kernel(meta, normed, weight, middle_gain, out_weight, *refs):
    gate, out_weights, middle, out_table, square = refs
    gate[...] = gate_of(normed, weight, 1)
    out_table[...] = out_weight[1].astype(F32)
    out_weights[...], middle[...] = output_weights(out_table, square, middle_gain[1:2, :], meta)


def outgoing_kernel(meta, *refs, rows, width):
    messages, outs = dict(zip(EVERYWHERE, refs[:8])), refs[8:12]
    left, right, total = refs[12:]
    dap, sub = meta[1] >> 1, meta[1] & 1
    lane = lane_index()
    count = outs[0].shape[0]
    span = 2 * rows
    pitch = span + GROUP

    @steps(rows // GROUP)
    def _(step):
        lanes = pl.ds(aligned(step * GROUP * width, LANES), GROUP * width)
        for k in range(8):
            values = messages[k][:, lanes].astype(F32)
            source = dap ^ (k >> 1)
            half = (source >> 1) ^ sub
            near = (source & 1) * rows
            if k < 4:
                begin = ((k >> 1) & 1) * rows + step * GROUP
                for c in range(0, count, GROUP):
                    for i, piece in enumerate(split_group(values[c : c + GROUP], width, lane)):
                        left[k & 1, pl.ds(c * pitch + begin + i, GROUP, stride=pitch), :] = piece
                values = values[count:]
            begin = half * (count * pitch) + near + step * GROUP
            for c in range(0, count, GROUP):
                for i, piece in enumerate(split_group(values[c : c + GROUP], width, lane)):
                    right[k & 1, pl.ds(c * pitch + begin + i, GROUP, stride=pitch), :] = piece

    @steps(count)
    def _(c):
        here = pl.ds(aligned(c * pitch, GROUP), span)
        a = jnp.concatenate([left[0, here, :], left[1, here, :]], axis=1).astype(BF16)
        for half in range(2):
            there = pl.ds(aligned(half * (count * pitch) + c * pitch, GROUP), span)
            b = jnp.concatenate([right[0, there, :], right[1, there, :]], axis=1).astype(BF16)
            total[half, here, 0:width] = lax.dot_general(
                a, b, (((1,), (1,)), ((), ())), preferred_element_type=F32
            )

    @steps(rows // GROUP)
    def _(step):
        lanes = pl.ds(aligned(step * GROUP * width, LANES), GROUP * width)
        for k in range(4):
            begin = (k >> 1) * rows + step * GROUP
            joined = []
            for c in range(0, count, GROUP):
                pieces = [
                    total[k & 1, pl.ds(c * pitch + begin + i, GROUP, stride=pitch), :]
                    for i in range(GROUP)
                ]
                joined.append(join_group(pieces, width, lane))
            outs[k][:, lanes] = jnp.concatenate(joined, axis=0).astype(BF16)


def incoming_kernel(meta, *refs, rows, width):
    messages, outs = dict(zip(WITHIN_HALF, refs[:4])), refs[4:12]
    left, right, total = refs[12:]
    dap, sub = meta[1] >> 1, meta[1] & 1
    lane = lane_index()
    count = outs[0].shape[0]
    span = 2 * rows
    pitch = span + GROUP
    tall = 2 * width
    tall_pitch = tall + GROUP

    @steps(rows // GROUP)
    def _(step):
        lanes = pl.ds(aligned(step * GROUP * width, LANES), GROUP * width)
        for k in range(4):
            values = messages[k][:, lanes].astype(F32)
            begin = (k >> 1) * rows + step * GROUP
            for side, part in ((left, values[:count]), (right, values[count:])):
                for c in range(0, count, GROUP):
                    for i, piece in enumerate(split_group(part[c : c + GROUP], width, lane)):
                        side[k & 1, pl.ds(c * pitch + begin + i, GROUP, stride=pitch), :] = piece

    @steps(count)
    def _(c):
        here = pl.ds(aligned(c * pitch, GROUP), span)
        b = jnp.concatenate([right[0, here, :], right[1, here, :]], axis=1).astype(BF16)
        for block in range(2):
            a = left[block, here, 0:width].astype(BF16)
            product = lax.dot_general(a, b, (((0,), (0,)), ((), ())), preferred_element_type=F32)
            there = pl.ds(aligned(c * tall_pitch + block * width, GROUP), width)
            total[0, there, :] = product[:, :LANES]
            total[1, there, :] = product[:, LANES:]

    @steps(rows // GROUP)
    def _(step):
        lanes = pl.ds(aligned(step * GROUP * width, LANES), GROUP * width)
        for k in range(8):
            target = dap ^ (k >> 1)
            begin = ((target >> 1) ^ sub) * width + (target & 1) * rows + step * GROUP
            joined = []
            for c in range(0, count, GROUP):
                pieces = [
                    total[k & 1, pl.ds(c * tall_pitch + begin + i, GROUP, stride=tall_pitch), :]
                    for i in range(GROUP)
                ]
                joined.append(join_group(pieces, width, lane))
            outs[k][:, lanes] = jnp.concatenate(joined, axis=0).astype(BF16)


def output_weights(table, square, gain, meta):
    core, chip = meta[0], meta[1]
    mine = table.shape[0] // 2
    size = mine // 4
    starts = [
        side * mine + size * ((chip & 3) ^ k) for side in (core, 1 - core) for k in range(4)
    ]
    square[...] = jnp.broadcast_to(gain, square.shape).T
    return pick_rows(table, starts, size).T.astype(BF16), pick_rows(square, starts, size)


def add_update(own, other, stream, gate, weights, factor, lanes):
    mixed = jnp.concatenate([own[:, lanes].astype(F32), other[:, lanes].astype(F32)], axis=0)
    middle = norm_rows(mixed, factor).astype(BF16)
    return stream[:, lanes] + gate[:, lanes] * jnp.dot(weights, middle, preferred_element_type=F32)


def second_kernel(
    own, other, stream, gate, mask, out_weights, middle, factor, weights, *refs, width
):
    stream_out, normed_out, *messages = refs
    channels = stream.shape[0]
    middles = jnp.concatenate([middle[...]] * (width // channels), axis=1)
    factors = jnp.concatenate([factor[...]] * (width // channels), axis=1)

    @blocks(stream.shape[1])
    def _(lanes):
        values = add_update(own, other, stream, gate, out_weights[...], middles, lanes)
        stream_out[:, lanes] = values
        normed = norm_rows(values, factors).astype(BF16)
        normed_out[:, lanes] = normed
        send_sides(normed, weights[...], mask[:, lanes], messages, lanes)


def last_scratch(channels, pairs):
    return [pltpu.VMEM((channels, pairs), F32)]


def last_kernel(
    meta, own, other, stream, gate, out_weights, middle, final_gain, expand, shrink, result, total
):
    first = meta[0] == 0
    rows, cols, channels = result.shape
    width = GROUP * 2 * cols
    middles = jnp.concatenate([middle[...]] * (width // channels), axis=1)

    @blocks(stream.shape[1])
    def _(lanes):
        total[:, lanes] = add_update(own, other, stream, gate, out_weights[...], middles, lanes)

    @steps(rows // GROUP)
    def _(step):
        values = total[:, pl.ds(step * width, width)].T.reshape(GROUP, 2 * cols, channels)
        flat = jnp.where(first, values[:, :cols], values[:, cols:]).reshape(GROUP * cols, channels)
        normed = layer_norm(flat, final_gain[...], 1).astype(BF16)
        expanded = jnp.dot(normed, expand[...], preferred_element_type=F32)
        expanded = jnp.maximum(expanded, 0.0).astype(BF16)
        out = flat + jnp.dot(expanded, shrink[...], preferred_element_type=F32)
        result[pl.ds(step * GROUP, GROUP)] = out.astype(BF16).reshape(GROUP, cols, channels)


def call(kernel, outs, scratch, args, scalars=1, flops=0):
    in_specs = [pl.BlockSpec(memory_space=pltpu.SMEM)] * scalars
    in_specs += [pl.BlockSpec(memory_space=pltpu.VMEM)] * (len(args) - scalars)
    moved = sum(a.size * a.dtype.itemsize for a in (*args, *outs))
    return pl.pallas_call(
        kernel,
        out_shape=outs,
        in_specs=in_specs,
        out_specs=[pl.BlockSpec(memory_space=pltpu.VMEM)] * len(outs),
        scratch_shapes=scratch,
        compiler_params=pltpu.CompilerParams(vmem_limit_bytes=40 * 1024 * 1024),
        cost_estimate=pl.CostEstimate(flops=flops, bytes_accessed=moved, transcendentals=0),
    )(*args)


def to_chip(value, distance):
    if distance == 0:
        return value
    pairs = [(device, device ^ (2 * distance)) for device in range(16)]
    return lax.ppermute(value, CHIPS, pairs)


def swap_cores(value):
    return lax.ppermute(value, "pair", [(0, 1), (1, 0)])


def chip_device(
    pair_input,
    residue_mask,
    entry_gain,
    input_weight,
    middle_gain,
    output_weight,
    final_gain,
    expand_weight,
    shrink_weight,
):
    rows, cols, channels = pair_input.shape
    hidden = output_weight.shape[1]
    width = 2 * cols
    pairs = rows * width
    wide = GROUP * width
    dap, sub, core = lax.axis_index("dap"), lax.axis_index("sub"), lax.axis_index("pair")
    meta = jnp.stack([core, dap * 2 + sub]).astype(jnp.int32)
    other_input = swap_cores(pair_input)
    shape = jax.ShapeDtypeStruct
    flat32, flat16 = shape((channels, pairs), F32), shape((channels, pairs), BF16)
    part = hidden // 8
    sides, rights = shape((2 * part, pairs), BF16), shape((part, pairs), BF16)
    span, tall = 2 * rows + GROUP, 2 * width + GROUP

    square32, square16 = shape((channels, channels), F32), shape((hidden, channels), BF16)
    side_weight = shape((2 * hidden, channels), BF16)
    mask_values = residue_mask.astype(F32)
    row_mask = lax.dynamic_slice_in_dim(mask_values, dap * rows, rows)
    col_mask = lax.dynamic_slice_in_dim(mask_values, sub * width, width)
    mask = (row_mask[:, None] * col_mask[None, :]).reshape(1, pairs)
    mask = jnp.concatenate([mask, entry_gain[0:1]], axis=1)

    stream, normed, *messages = call(
        first_kernel,
        [flat32, flat16] + [sides] * 4 + [rights] * 4,
        [pltpu.VMEM((4 * hidden, channels), F32)],
        (meta, pair_input, other_input, mask, input_weight[0, :, : 4 * hidden]),
    )
    arrived = [to_chip(messages[k], k) for k in EVERYWHERE]
    gate, out_weights, middle, factor, weights = call(
        first_gate_kernel,
        [flat32, square16, square32, square32, side_weight],
        [
            pltpu.VMEM((4 * hidden, channels), F32),
            pltpu.VMEM((hidden, channels), F32),
            pltpu.VMEM((hidden, LANES), F32),
        ],
        (meta, normed, input_weight, entry_gain, middle_gain, output_weight),
    )
    sums = call(
        functools.partial(outgoing_kernel, rows=rows, width=width),
        [rights] * 4,
        [
            pltpu.VMEM((2, part * span, LANES), F32),
            pltpu.VMEM((2, 2 * part * span, LANES), F32),
            pltpu.VMEM((2, part * span, LANES), F32),
        ],
        (meta, *arrived),
    )
    returned = [to_chip(sums[k], k) for k in WITHIN_HALF]
    own = jnp.concatenate(returned[::-1], axis=0)
    other = swap_cores(own)
    stream, normed, *messages = call(
        functools.partial(second_kernel, width=wide),
        [flat32, flat16] + [sides] * 4,
        [],
        (own, other, stream, gate, mask, out_weights, middle, factor, weights),
        0,
    )
    arrived = [to_chip(messages[k], k) for k in WITHIN_HALF]
    gate, out_weights, middle = call(
        second_gate_kernel,
        [flat32, square16, square32],
        [pltpu.VMEM((hidden, channels), F32), pltpu.VMEM((hidden, LANES), F32)],
        (meta, normed, input_weight, middle_gain, output_weight),
    )
    sums = call(
        functools.partial(incoming_kernel, rows=rows, width=width),
        [rights] * 8,
        [
            pltpu.VMEM((2, part * span, LANES), F32),
            pltpu.VMEM((2, part * span, LANES), F32),
            pltpu.VMEM((2, part * tall, LANES), F32),
        ],
        (meta, *arrived),
    )
    returned = {k: to_chip(sums[k], k) for k in EVERYWHERE}
    near = jnp.concatenate([returned[k] for k in range(4)], axis=0)
    far = jnp.concatenate([returned[4 + k] for k in range(4)], axis=0)
    own = (near.astype(F32) + far.astype(F32)).astype(BF16)
    other = swap_cores(own)
    (result,) = call(
        last_kernel,
        [shape((rows, cols, channels), BF16)],
        last_scratch(channels, pairs),
        (
            meta, own, other, stream, gate, out_weights, middle,
            final_gain.reshape(1, channels), expand_weight, shrink_weight,
        ),
    )
    return result


def by_chips(mesh, pair_input, output_weight):
    sizes = dict(mesh.shape)
    rows = pair_input.shape[0] // (sizes["grp"] * sizes["dap"])
    cols = pair_input.shape[1] // (sizes["sub"] * sizes["pair"])
    return (
        (sizes["dap"], sizes["sub"], sizes["pair"]) == (4, 2, 2)
        and pair_input.shape[2] == LANES
        and output_weight.shape[1] == LANES
        and rows == cols
        and rows % GROUP == 0
        and 2 * cols <= LANES
        and GROUP * 2 * cols % LANES == 0
    )


def solution(mesh):
    placed = (P(("grp", "dap"), ("sub", "pair"), None), P("grp"), P(), P(), P(), P(), P(), P(), P())

    def run(*args):
        fits = by_chips(mesh, args[0], args[5])
        return jax.shard_map(
            chip_device if fits else general_device,
            mesh=mesh,
            in_specs=placed,
            out_specs=P(("grp", "dap"), ("sub", "pair"), None),
            check_vma=False,
        )(*args)

    return run
```

```python
import functools

import jax
import jax.numpy as jnp
from jax import lax
from jax.experimental import pallas as pl
from jax.experimental.pallas import tpu as pltpu
from jax.sharding import PartitionSpec as P

F32 = jnp.float32
BF16 = jnp.bfloat16
LANES = 128
GROUP = 8
CHIPS = ("dap", "sub", "pair")


def layer_norm(values, factor, dimension):
    average = jnp.mean(values, axis=dimension, keepdims=True)
    centred = values - average
    variance = jnp.mean(centred * centred, axis=dimension, keepdims=True)
    return centred * lax.rsqrt(variance + 1e-05) * factor


def spread_rows(left_side, right_side):
    return (
        lax.all_to_all(left_side, ("sub", "pair"), split_axis=0, concat_axis=2, tiled=True),
        lax.all_to_all(right_side, ("sub", "pair"), split_axis=0, concat_axis=2, tiled=True),
    )


def return_rows(mixed_sum):
    return lax.all_to_all(mixed_sum, ("sub", "pair"), split_axis=2, concat_axis=0, tiled=True)


def outgoing_rows(left_side, right_side):
    left_wide, right_wide = spread_rows(left_side, right_side)
    summed = jnp.einsum(
        "cik,cjk->cij",
        left_wide,
        lax.all_gather(right_wide, "dap", axis=1, tiled=True),
        preferred_element_type=jnp.float32,
    )
    return return_rows(summed.astype(jnp.bfloat16))


def incoming_rows(left_side, right_side):
    left_wide, right_wide = spread_rows(left_side, right_side)
    flipped = lax.all_to_all(left_wide, "dap", split_axis=2, concat_axis=1, tiled=True)
    summed = jnp.einsum(
        "cki,ckj->cij",
        flipped,
        lax.all_gather(right_wide, "dap", axis=1, tiled=True),
        preferred_element_type=jnp.float32,
    )
    return return_rows(summed.astype(jnp.bfloat16))


def triangle_update(
    stream, pair_mask, entry_gain, input_weight, middle_gain, output_weight, incoming
):
    row_count, col_count, channels = stream.shape
    hidden = output_weight.shape[0]
    normed = (
        layer_norm(stream, entry_gain, 2)
        .astype(jnp.bfloat16)
        .reshape(row_count * col_count, channels)
    )
    projected = lax.dot_general(
        input_weight[:, : 4 * hidden],
        normed,
        (((0,), (1,)), ((), ())),
        preferred_element_type=jnp.float32,
    )
    projected = projected.reshape(4 * hidden, row_count, col_count)
    left_side = (
        pair_mask * jax.nn.sigmoid(projected[hidden : 2 * hidden]) * projected[:hidden]
    ).astype(jnp.bfloat16)
    right_side = (
        pair_mask * jax.nn.sigmoid(projected[3 * hidden :]) * projected[2 * hidden : 3 * hidden]
    ).astype(jnp.bfloat16)
    gate_vals = jax.nn.sigmoid(
        jnp.dot(normed, input_weight[:, 4 * hidden :], preferred_element_type=jnp.float32)
    )
    mixed_sum = (
        incoming_rows(left_side, right_side) if incoming else outgoing_rows(left_side, right_side)
    )
    middle = layer_norm(mixed_sum.astype(jnp.float32), middle_gain[:, None, None], 0).astype(
        jnp.bfloat16
    )
    middle = middle.reshape(hidden, row_count * col_count)
    output = lax.dot_general(
        middle, output_weight, (((0,), (0,)), ((), ())), preferred_element_type=jnp.float32
    )
    return stream + (gate_vals * output).reshape(row_count, col_count, channels)


def general_device(
    pair_input,
    residue_mask,
    entry_gain,
    input_weight,
    middle_gain,
    output_weight,
    final_gain,
    expand_weight,
    shrink_weight,
):
    row_count, col_count, channels = pair_input.shape
    row_offset = lax.axis_index("dap") * row_count
    col_offset = lax.axis_index(("sub", "pair")) * col_count
    row_mask = lax.dynamic_slice_in_dim(residue_mask, row_offset, row_count).astype(jnp.float32)
    col_mask = lax.dynamic_slice_in_dim(residue_mask, col_offset, col_count).astype(jnp.float32)
    pair_mask = row_mask[:, None] * col_mask[None, :]
    stream = pair_input.astype(jnp.float32)
    for update_id in range(2):
        stream = triangle_update(
            stream,
            pair_mask,
            entry_gain[update_id],
            input_weight[update_id],
            middle_gain[update_id],
            output_weight[update_id],
            update_id == 1,
        )
    flat = stream.reshape(row_count * col_count, channels)
    normed = layer_norm(flat, final_gain, 1).astype(jnp.bfloat16)
    expanded = jax.nn.relu(
        jnp.dot(normed, expand_weight, preferred_element_type=jnp.float32)
    ).astype(jnp.bfloat16)
    result = flat + jnp.dot(expanded, shrink_weight, preferred_element_type=jnp.float32)
    return result.astype(jnp.bfloat16).reshape(row_count, col_count, channels)


FIRST_ORDER = (4, 5, 2, 6, 3, 7, 1, 0)
LAST_ORDER = (4, 2, 5, 3, 6, 1, 7, 0)
WITHIN_HALF = (3, 2, 1, 0)


def aligned(start, size):
    return start if isinstance(start, int) else pl.multiple_of(start, size)


def steps(count):
    def run(body):
        for step in range(count):
            body(step)

    return run


def blocks(count, size=2 * LANES):
    def run(body):
        for begin in range(0, count, size):
            body(slice(begin, min(begin + size, count)))

    return run


def sigmoid(values):
    return 0.5 * jnp.tanh(0.5 * values) + 0.5


def norm_rows(values, factor):
    return jnp.concatenate(
        [
            norm_block(values[:, b : b + LANES], factor[:, :LANES])
            for b in range(0, values.shape[1], LANES)
        ],
        axis=1,
    )


def norm_block(values, factor):
    average = jnp.mean(values, axis=0, keepdims=True)
    centred = values - average
    variance = jnp.mean(centred * centred, axis=0, keepdims=True)
    return centred * lax.rsqrt(variance + 1e-05) * factor


def column_of(gain_row, width):
    square = jnp.broadcast_to(gain_row, (gain_row.shape[1], gain_row.shape[1])).T
    return jnp.concatenate([square] * (width // square.shape[1]), axis=1)


def lane_index():
    return lax.broadcasted_iota(jnp.int32, (GROUP, LANES), 1)


def split_group(chunk, width):
    lane = lane_index()
    pieces = []
    for row in range(GROUP):
        first, offset = divmod(row * width, LANES)
        piece = chunk[:, first * LANES : (first + 1) * LANES]
        if offset:
            piece = pltpu.roll(piece, LANES - offset, 1)
            if offset + width > LANES:
                after = chunk[:, (first + 1) * LANES : (first + 2) * LANES]
                after = pltpu.roll(after, LANES - offset, 1)
                piece = jnp.where(lane < LANES - offset, piece, after)
        pieces.append(piece)
    return pieces


def join_group(pieces, width, lane):
    parts = []
    for part in range(GROUP * width // LANES):
        begin = part * LANES
        value = None
        for row in range(begin // width, (begin + LANES - 1) // width + 1):
            shift = row * width - begin
            piece = pieces[row]
            if shift % LANES:
                piece = pltpu.roll(piece, shift % LANES, 1)
            value = piece if value is None else jnp.where(lane >= shift, piece, value)
        parts.append(value)
    return jnp.concatenate(parts, axis=1)


def pick_rows(table, starts, size):
    return jnp.concatenate(
        [table[pl.ds(aligned(start, GROUP), size), :] for start in starts], axis=0
    )


def side_weights(table, meta):
    core, chip = meta[0], meta[1]
    hidden = table.shape[0] // 4
    mine = hidden // 2
    size = mine // 4
    picked = []
    for base in range(4):
        starts = [base * hidden + core * mine + size * ((chip & 3) ^ k) for k in range(4)]
        picked.append(pick_rows(table, starts, size))
    return jnp.concatenate(picked, axis=0).astype(BF16)


def send_sides(normed, weights, messages, lanes):
    quarter = weights.shape[0] // 4
    projected = jnp.dot(weights, normed, preferred_element_type=F32)
    left = sigmoid(projected[quarter : 2 * quarter]) * projected[:quarter]
    right = sigmoid(projected[3 * quarter :]) * projected[2 * quarter : 3 * quarter]
    size = quarter // 4
    for k in range(4):
        rows = slice(k * size, (k + 1) * size)
        messages[k][:, lanes] = jnp.concatenate([left[rows], right[rows]], axis=0).astype(BF16)
        if len(messages) > 4:
            messages[4 + k][:, lanes] = right[rows].astype(BF16)


def pick_columns(first, own, other):
    return jnp.where(
        first, jnp.concatenate([own, other], axis=1), jnp.concatenate([other, own], axis=1)
    )


def first_kernel(meta, own, other, gain, weight, *refs):
    stream, normed_out, *messages, table = refs
    first = meta[0] == 0
    rows, cols, channels = own.shape
    width = GROUP * 2 * cols
    factors = column_of(gain[...], channels)
    table[...] = weight[...].astype(F32).T
    weights = side_weights(table, meta)

    @steps(rows // GROUP)
    def _(step):
        lanes = pl.ds(step * width, width)
        here = pl.ds(step * GROUP, GROUP)
        values = pick_columns(first, own[here].astype(F32), other[here].astype(F32))
        values = values.reshape(width, channels).T
        stream[:, lanes] = values

    @blocks(stream.shape[1])
    def _(lanes):
        normed = norm_rows(stream[:, lanes], factors).astype(BF16)
        normed_out[:, lanes] = normed
        send_sides(normed, weights, messages, lanes)


def gate_of(normed, weight, update):
    channels = normed.shape[0]
    hidden = (weight.shape[2] - channels) // 4
    table = weight[update, :, 4 * hidden :].astype(F32).T.astype(BF16)
    return sigmoid(jnp.dot(table, normed[...], preferred_element_type=F32))


def chip_masks(bits, column, meta, masks, width):
    dap, sub = meta[1] >> 1, meta[1] & 1
    rows = masks.shape[1]
    values = bits[...].astype(F32)
    column[...] = jnp.broadcast_to(values, (LANES, values.shape[1])).T
    parts = [values[:, b * width : (b + 1) * width] for b in range(2)]
    parts = [jnp.concatenate([p, jnp.zeros((1, LANES - width), F32)], axis=1) for p in parts]
    for k in range(8):
        begin = aligned((dap ^ (k >> 1)) * rows, GROUP)
        masks[k] = column[pl.ds(begin, rows), :] * jnp.where(sub == (k & 1), parts[0], parts[1])


def first_gate_kernel(meta, normed, weight, entry_gain, middle_gain, out_weight, bits, *refs):
    gate, out_weights, middle, factor, weights, masks, table, out_table, square, column = refs
    chip_masks(bits, column, meta, masks, bits.shape[1] // 2)
    gate[...] = gate_of(normed, weight, 0)
    out_table[...] = out_weight[0].astype(F32)
    out_weights[...], middle[...] = output_weights(out_table, square, middle_gain[0:1, :], meta)
    factor[...] = column_of(entry_gain[1:2, :], factor.shape[1])
    table[...] = weight[1, :, : table.shape[0]].astype(F32).T
    weights[...] = side_weights(table, meta)


def second_gate_kernel(meta, normed, weight, middle_gain, out_weight, *refs):
    gate, out_weights, middle, out_table, square = refs
    gate[...] = gate_of(normed, weight, 1)
    out_table[...] = out_weight[1].astype(F32)
    out_weights[...], middle[...] = output_weights(out_table, square, middle_gain[1:2, :], meta)


def spread_group(side, part, masks, begin, pitch, width):
    for c in range(0, part.shape[0], GROUP):
        for i, piece in enumerate(split_group(part[c : c + GROUP], width)):
            side[pl.ds(c * pitch + begin + i, GROUP, stride=pitch), :] = piece * masks[i : i + 1]


def gather_group(total, count, begin, pitch, width, lane):
    joined = []
    for c in range(0, count, GROUP):
        pieces = [
            total[pl.ds(c * pitch + begin + i, GROUP, stride=pitch), :] for i in range(GROUP)
        ]
        joined.append(join_group(pieces, width, lane))
    return jnp.concatenate(joined, axis=0).astype(BF16)


def outgoing_kernel(meta, masks, *refs, rows, width):
    messages, outs = dict(zip(FIRST_ORDER, refs[:8])), refs[8:12]
    left, right, total = refs[12:]
    dap, sub = meta[1] >> 1, meta[1] & 1
    lane = lane_index()
    count = outs[0].shape[0]
    span = 2 * rows
    pitch = span + GROUP

    @steps(rows // GROUP)
    def _(step):
        lanes = pl.ds(step * GROUP * width, GROUP * width)
        for k in range(8):
            values = messages[k][:, lanes].astype(F32)
            bits = masks[k, step * GROUP : (step + 1) * GROUP, :]
            if k < 4:
                begin = (k >> 1) * rows + step * GROUP
                spread_group(left.at[k & 1], values[:count], bits, begin, pitch, width)
                values = values[count:]
            source = dap ^ (k >> 1)
            begin = ((source >> 1) ^ sub) * (count * pitch) + (source & 1) * rows + step * GROUP
            spread_group(right.at[k & 1], values, bits, begin, pitch, width)

    for c in range(count):
        here = pl.ds(c * pitch, span)
        a = jnp.concatenate([left[0, here, :], left[1, here, :]], axis=1).astype(BF16)
        for half in range(2):
            there = pl.ds((half * count + c) * pitch, span)
            b = jnp.concatenate([right[0, there, :], right[1, there, :]], axis=1).astype(BF16)
            total[half, here, 0:width] = lax.dot_general(
                a, b, (((1,), (1,)), ((), ())), preferred_element_type=F32
            )

    @steps(rows // GROUP)
    def _(step):
        lanes = pl.ds(step * GROUP * width, GROUP * width)
        for k in range(4):
            begin = (k >> 1) * rows + step * GROUP
            outs[k][:, lanes] = gather_group(total.at[k & 1], count, begin, pitch, width, lane)


def incoming_kernel(meta, masks, *refs, rows, width):
    messages, outs = dict(zip(WITHIN_HALF, refs[:4])), refs[4:12]
    left, right, total = refs[12:]
    dap, sub = meta[1] >> 1, meta[1] & 1
    lane = lane_index()
    count = outs[0].shape[0]
    span = 2 * rows
    pitch = span + GROUP
    tall = 2 * width + GROUP

    @steps(rows // GROUP)
    def _(step):
        lanes = pl.ds(step * GROUP * width, GROUP * width)
        for k in range(4):
            values = messages[k][:, lanes].astype(F32)
            bits = masks[k, step * GROUP : (step + 1) * GROUP, :]
            begin = (k >> 1) * rows + step * GROUP
            spread_group(left.at[k & 1], values[:count], bits, begin, pitch, width)
            spread_group(right.at[k & 1], values[count:], bits, begin, pitch, width)

    for c in range(count):
        here = pl.ds(c * pitch, span)
        b = jnp.concatenate([right[0, here, :], right[1, here, :]], axis=1).astype(BF16)
        for block in range(2):
            a = left[block, here, 0:width].astype(BF16)
            product = lax.dot_general(a, b, (((0,), (0,)), ((), ())), preferred_element_type=F32)
            there = pl.ds(c * tall + block * width, width)
            total[0, there, :] = product[:, :LANES]
            total[1, there, :] = product[:, LANES:]

    @steps(rows // GROUP)
    def _(step):
        lanes = pl.ds(step * GROUP * width, GROUP * width)
        for k in range(8):
            target = dap ^ (k >> 1)
            begin = ((target >> 1) ^ sub) * width + (target & 1) * rows + step * GROUP
            outs[k][:, lanes] = gather_group(total.at[k & 1], count, begin, tall, width, lane)


def output_weights(table, square, gain, meta):
    core, chip = meta[0], meta[1]
    mine = table.shape[0] // 2
    size = mine // 4
    starts = [
        side * mine + size * ((chip & 3) ^ k) for side in (core, 1 - core) for k in range(4)
    ]
    square[...] = jnp.broadcast_to(gain, square.shape).T
    return pick_rows(table, starts, size).T.astype(BF16), pick_rows(square, starts, size)


def add_update(own, other, stream, gate, weights, factor, lanes):
    mixed = jnp.concatenate([own[:, lanes].astype(F32), other[:, lanes].astype(F32)], axis=0)
    middle = norm_rows(mixed, factor).astype(BF16)
    return stream[:, lanes] + gate[:, lanes] * jnp.dot(weights, middle, preferred_element_type=F32)


def second_kernel(
    own, other, stream, gate, out_weights, middle, factor, weights, *refs, width
):
    stream_out, normed_out, *messages = refs
    channels = stream.shape[0]
    middles = jnp.concatenate([middle[...]] * (width // channels), axis=1)
    factors = jnp.concatenate([factor[...]] * (width // channels), axis=1)

    @blocks(stream.shape[1])
    def _(lanes):
        values = add_update(own, other, stream, gate, out_weights[...], middles, lanes)
        stream_out[:, lanes] = values
        normed = norm_rows(values, factors).astype(BF16)
        normed_out[:, lanes] = normed
        send_sides(normed, weights[...], messages, lanes)


def last_scratch(channels, pairs):
    return [pltpu.VMEM((channels, pairs), F32)]


def last_kernel(
    meta, own, other, stream, gate, out_weights, middle, final_gain, expand, shrink, result, total
):
    first = meta[0] == 0
    rows, cols, channels = result.shape
    width = GROUP * 2 * cols
    middles = jnp.concatenate([middle[...]] * (width // channels), axis=1)

    @blocks(stream.shape[1])
    def _(lanes):
        total[:, lanes] = add_update(own, other, stream, gate, out_weights[...], middles, lanes)

    @steps(rows // GROUP)
    def _(step):
        values = total[:, pl.ds(step * width, width)].T.reshape(GROUP, 2 * cols, channels)
        flat = jnp.where(first, values[:, :cols], values[:, cols:]).reshape(GROUP * cols, channels)
        normed = layer_norm(flat, final_gain[...], 1).astype(BF16)
        expanded = jnp.dot(normed, expand[...], preferred_element_type=F32)
        expanded = jnp.maximum(expanded, 0.0).astype(BF16)
        out = flat + jnp.dot(expanded, shrink[...], preferred_element_type=F32)
        result[pl.ds(step * GROUP, GROUP)] = out.astype(BF16).reshape(GROUP, cols, channels)


def call(kernel, outs, scratch, args, scalars=1, flops=0):
    in_specs = [pl.BlockSpec(memory_space=pltpu.SMEM)] * scalars
    in_specs += [pl.BlockSpec(memory_space=pltpu.VMEM)] * (len(args) - scalars)
    moved = sum(a.size * a.dtype.itemsize for a in (*args, *outs))
    return pl.pallas_call(
        kernel,
        out_shape=outs,
        in_specs=in_specs,
        out_specs=[pl.BlockSpec(memory_space=pltpu.VMEM)] * len(outs),
        scratch_shapes=scratch,
        compiler_params=pltpu.CompilerParams(vmem_limit_bytes=40 * 1024 * 1024),
        cost_estimate=pl.CostEstimate(flops=flops, bytes_accessed=moved, transcendentals=0),
    )(*args)


def to_chip(value, distance):
    if distance == 0:
        return value
    pairs = [(device, device ^ (2 * distance)) for device in range(16)]
    return lax.ppermute(value, CHIPS, pairs)


def swap_cores(value):
    return lax.ppermute(value, "pair", [(0, 1), (1, 0)])


def chip_device(
    pair_input,
    residue_mask,
    entry_gain,
    input_weight,
    middle_gain,
    output_weight,
    final_gain,
    expand_weight,
    shrink_weight,
):
    rows, cols, channels = pair_input.shape
    hidden = output_weight.shape[1]
    width = 2 * cols
    pairs = rows * width
    wide = GROUP * width
    dap, sub, core = lax.axis_index("dap"), lax.axis_index("sub"), lax.axis_index("pair")
    meta = jnp.stack([core, dap * 2 + sub]).astype(jnp.int32)
    other_input = swap_cores(pair_input)
    shape = jax.ShapeDtypeStruct
    flat32, flat16 = shape((channels, pairs), F32), shape((channels, pairs), BF16)
    part = hidden // 8
    sides, rights = shape((2 * part, pairs), BF16), shape((part, pairs), BF16)
    span, tall = 2 * rows + GROUP, 2 * width + GROUP

    square32, square16 = shape((channels, channels), F32), shape((hidden, channels), BF16)
    side_weight = shape((2 * hidden, channels), BF16)
    stream, normed, *messages = call(
        first_kernel,
        [flat32, flat16] + [sides] * 4 + [rights] * 4,
        [pltpu.VMEM((4 * hidden, channels), F32)],
        (meta, pair_input, other_input, entry_gain[0:1], input_weight[0, :, : 4 * hidden]),
    )
    arrived = [to_chip(messages[k], k) for k in FIRST_ORDER]
    length = residue_mask.shape[0]
    gate, out_weights, middle, factor, weights, masks = call(
        first_gate_kernel,
        [flat32, square16, square32, square32, side_weight, shape((8, rows, LANES), F32)],
        [
            pltpu.VMEM((4 * hidden, channels), F32),
            pltpu.VMEM((hidden, channels), F32),
            pltpu.VMEM((hidden, LANES), F32),
            pltpu.VMEM((length, LANES), F32),
        ],
        (
            meta, normed, input_weight, entry_gain, middle_gain, output_weight,
            residue_mask.reshape(1, length),
        ),
    )
    sums = call(
        functools.partial(outgoing_kernel, rows=rows, width=width),
        [rights] * 4,
        [
            pltpu.VMEM((2, part * span, LANES), F32),
            pltpu.VMEM((2, 2 * part * span, LANES), F32),
            pltpu.VMEM((2, part * span, LANES), F32),
        ],
        (meta, masks, *arrived),
    )
    returned = [to_chip(sums[k], k) for k in WITHIN_HALF]
    own = jnp.concatenate(returned[::-1], axis=0)
    other = swap_cores(own)
    stream, normed, *messages = call(
        functools.partial(second_kernel, width=wide),
        [flat32, flat16] + [sides] * 4,
        [],
        (own, other, stream, gate, out_weights, middle, factor, weights),
        0,
    )
    arrived = [to_chip(messages[k], k) for k in WITHIN_HALF]
    gate, out_weights, middle = call(
        second_gate_kernel,
        [flat32, square16, square32],
        [pltpu.VMEM((hidden, channels), F32), pltpu.VMEM((hidden, LANES), F32)],
        (meta, normed, input_weight, middle_gain, output_weight),
    )
    sums = call(
        functools.partial(incoming_kernel, rows=rows, width=width),
        [rights] * 8,
        [
            pltpu.VMEM((2, part * span, LANES), F32),
            pltpu.VMEM((2, part * span, LANES), F32),
            pltpu.VMEM((2, part * tall, LANES), F32),
        ],
        (meta, masks, *arrived),
    )
    returned = {k: to_chip(sums[k], k) for k in LAST_ORDER}
    near = jnp.concatenate([returned[k] for k in range(4)], axis=0)
    far = jnp.concatenate([returned[4 + k] for k in range(4)], axis=0)
    own = (near.astype(F32) + far.astype(F32)).astype(BF16)
    other = swap_cores(own)
    (result,) = call(
        last_kernel,
        [shape((rows, cols, channels), BF16)],
        last_scratch(channels, pairs),
        (
            meta, own, other, stream, gate, out_weights, middle,
            final_gain.reshape(1, channels), expand_weight, shrink_weight,
        ),
    )
    return result


def by_chips(mesh, pair_input, output_weight):
    sizes = dict(mesh.shape)
    rows = pair_input.shape[0] // (sizes["grp"] * sizes["dap"])
    cols = pair_input.shape[1] // (sizes["sub"] * sizes["pair"])
    return (
        (sizes["dap"], sizes["sub"], sizes["pair"]) == (4, 2, 2)
        and pair_input.shape[2] == LANES
        and output_weight.shape[1] == LANES
        and rows == cols
        and rows % GROUP == 0
        and 2 * cols <= LANES
        and GROUP * 2 * cols % LANES == 0
    )


def solution(mesh):
    placed = (P(("grp", "dap"), ("sub", "pair"), None), P("grp"), P(), P(), P(), P(), P(), P(), P())

    def run(*args):
        fits = by_chips(mesh, args[0], args[5])
        return jax.shard_map(
            chip_device if fits else general_device,
            mesh=mesh,
            in_specs=placed,
            out_specs=P(("grp", "dap"), ("sub", "pair"), None),
            check_vma=False,
        )(*args)

    return run
```

```python
import functools

import jax
import jax.numpy as jnp
from jax import lax
from jax.experimental import pallas as pl
from jax.experimental.pallas import tpu as pltpu
from jax.sharding import PartitionSpec as P

F32 = jnp.float32
BF16 = jnp.bfloat16
LANES = 128
GROUP = 8
CHIPS = ("dap", "sub", "pair")


def layer_norm(values, factor, dimension):
    average = jnp.mean(values, axis=dimension, keepdims=True)
    centred = values - average
    variance = jnp.mean(centred * centred, axis=dimension, keepdims=True)
    return centred * lax.rsqrt(variance + 1e-05) * factor


def spread_rows(left_side, right_side):
    return (
        lax.all_to_all(left_side, ("sub", "pair"), split_axis=0, concat_axis=2, tiled=True),
        lax.all_to_all(right_side, ("sub", "pair"), split_axis=0, concat_axis=2, tiled=True),
    )


def return_rows(mixed_sum):
    return lax.all_to_all(mixed_sum, ("sub", "pair"), split_axis=2, concat_axis=0, tiled=True)


def outgoing_rows(left_side, right_side):
    left_wide, right_wide = spread_rows(left_side, right_side)
    summed = jnp.einsum(
        "cik,cjk->cij",
        left_wide,
        lax.all_gather(right_wide, "dap", axis=1, tiled=True),
        preferred_element_type=jnp.float32,
    )
    return return_rows(summed.astype(jnp.bfloat16))


def incoming_rows(left_side, right_side):
    left_wide, right_wide = spread_rows(left_side, right_side)
    flipped = lax.all_to_all(left_wide, "dap", split_axis=2, concat_axis=1, tiled=True)
    summed = jnp.einsum(
        "cki,ckj->cij",
        flipped,
        lax.all_gather(right_wide, "dap", axis=1, tiled=True),
        preferred_element_type=jnp.float32,
    )
    return return_rows(summed.astype(jnp.bfloat16))


def triangle_update(
    stream, pair_mask, entry_gain, input_weight, middle_gain, output_weight, incoming
):
    row_count, col_count, channels = stream.shape
    hidden = output_weight.shape[0]
    normed = (
        layer_norm(stream, entry_gain, 2)
        .astype(jnp.bfloat16)
        .reshape(row_count * col_count, channels)
    )
    projected = lax.dot_general(
        input_weight[:, : 4 * hidden],
        normed,
        (((0,), (1,)), ((), ())),
        preferred_element_type=jnp.float32,
    )
    projected = projected.reshape(4 * hidden, row_count, col_count)
    left_side = (
        pair_mask * jax.nn.sigmoid(projected[hidden : 2 * hidden]) * projected[:hidden]
    ).astype(jnp.bfloat16)
    right_side = (
        pair_mask * jax.nn.sigmoid(projected[3 * hidden :]) * projected[2 * hidden : 3 * hidden]
    ).astype(jnp.bfloat16)
    gate_vals = jax.nn.sigmoid(
        jnp.dot(normed, input_weight[:, 4 * hidden :], preferred_element_type=jnp.float32)
    )
    mixed_sum = (
        incoming_rows(left_side, right_side) if incoming else outgoing_rows(left_side, right_side)
    )
    middle = layer_norm(mixed_sum.astype(jnp.float32), middle_gain[:, None, None], 0).astype(
        jnp.bfloat16
    )
    middle = middle.reshape(hidden, row_count * col_count)
    output = lax.dot_general(
        middle, output_weight, (((0,), (0,)), ((), ())), preferred_element_type=jnp.float32
    )
    return stream + (gate_vals * output).reshape(row_count, col_count, channels)


def general_device(
    pair_input,
    residue_mask,
    entry_gain,
    input_weight,
    middle_gain,
    output_weight,
    final_gain,
    expand_weight,
    shrink_weight,
):
    row_count, col_count, channels = pair_input.shape
    row_offset = lax.axis_index("dap") * row_count
    col_offset = lax.axis_index(("sub", "pair")) * col_count
    row_mask = lax.dynamic_slice_in_dim(residue_mask, row_offset, row_count).astype(jnp.float32)
    col_mask = lax.dynamic_slice_in_dim(residue_mask, col_offset, col_count).astype(jnp.float32)
    pair_mask = row_mask[:, None] * col_mask[None, :]
    stream = pair_input.astype(jnp.float32)
    for update_id in range(2):
        stream = triangle_update(
            stream,
            pair_mask,
            entry_gain[update_id],
            input_weight[update_id],
            middle_gain[update_id],
            output_weight[update_id],
            update_id == 1,
        )
    flat = stream.reshape(row_count * col_count, channels)
    normed = layer_norm(flat, final_gain, 1).astype(jnp.bfloat16)
    expanded = jax.nn.relu(
        jnp.dot(normed, expand_weight, preferred_element_type=jnp.float32)
    ).astype(jnp.bfloat16)
    result = flat + jnp.dot(expanded, shrink_weight, preferred_element_type=jnp.float32)
    return result.astype(jnp.bfloat16).reshape(row_count, col_count, channels)


FIRST_ORDER = (4, 5, 2, 6, 3, 7, 1, 0)
LAST_ORDER = (4, 2, 5, 3, 6, 1, 7, 0)
WITHIN_HALF = (3, 2, 1, 0)
SIDES_WITHIN = (2, 3, 1, 0)


def aligned(start, size):
    return start if isinstance(start, int) else pl.multiple_of(start, size)


def steps(count):
    def run(body):
        for step in range(count):
            body(step)

    return run


def blocks(count, size=2 * LANES):
    def run(body):
        for begin in range(0, count, size):
            body(slice(begin, min(begin + size, count)))

    return run


def sigmoid_of_double(values):
    return 0.5 * jnp.tanh(values) + 0.5


def norm_rows(values, factor):
    return jnp.concatenate(
        [
            norm_block(values[:, b : b + LANES], factor[:, :LANES])
            for b in range(0, values.shape[1], LANES)
        ],
        axis=1,
    )


def norm_block(values, factor):
    average = jnp.mean(values, axis=0, keepdims=True)
    centred = values - average
    variance = jnp.mean(centred * centred, axis=0, keepdims=True)
    return centred * lax.rsqrt(variance + 1e-05) * factor


def column_of(gain_row, width):
    square = jnp.broadcast_to(gain_row, (gain_row.shape[1], gain_row.shape[1])).T
    return jnp.concatenate([square] * (width // square.shape[1]), axis=1)


def lane_index():
    return lax.broadcasted_iota(jnp.int32, (GROUP, LANES), 1)


def split_group(chunk, width):
    lane = lane_index()
    pieces = []
    for row in range(GROUP):
        first, offset = divmod(row * width, LANES)
        piece = chunk[:, first * LANES : (first + 1) * LANES]
        if offset:
            piece = pltpu.roll(piece, LANES - offset, 1)
            if offset + width > LANES:
                after = chunk[:, (first + 1) * LANES : (first + 2) * LANES]
                after = pltpu.roll(after, LANES - offset, 1)
                piece = jnp.where(lane < LANES - offset, piece, after)
        pieces.append(piece)
    return pieces


def join_group(pieces, width, lane):
    parts = []
    for part in range(GROUP * width // LANES):
        begin = part * LANES
        value = None
        for row in range(begin // width, (begin + LANES - 1) // width + 1):
            shift = row * width - begin
            piece = pieces[row]
            if shift % LANES:
                piece = pltpu.roll(piece, shift % LANES, 1)
            value = piece if value is None else jnp.where(lane >= shift, piece, value)
        parts.append(value)
    return jnp.concatenate(parts, axis=1)


def pick_rows(table, starts, size):
    return jnp.concatenate(
        [table[pl.ds(aligned(start, GROUP), size), :] for start in starts], axis=0
    )


def side_weights(table, meta):
    core, chip = meta[0], meta[1]
    hidden = table.shape[0] // 4
    mine = hidden // 2
    size = mine // 4
    picked = []
    for base in range(4):
        starts = [base * hidden + core * mine + size * ((chip & 3) ^ k) for k in range(4)]
        picked.append(pick_rows(table, starts, size))
    return (0.5 * jnp.concatenate(picked, axis=0)).astype(BF16)


def send_sides(normed, weights, messages, lanes):
    quarter = weights.shape[0] // 4
    projected = jnp.dot(weights, normed, preferred_element_type=F32)
    left = (jnp.tanh(projected[quarter : 2 * quarter]) + 1.0) * projected[:quarter]
    right = (jnp.tanh(projected[3 * quarter :]) + 1.0) * projected[2 * quarter : 3 * quarter]
    size = quarter // 4
    for k in range(4):
        rows = slice(k * size, (k + 1) * size)
        messages[k][:, lanes] = jnp.concatenate([left[rows], right[rows]], axis=0).astype(BF16)
        if len(messages) > 4:
            messages[4 + k][:, lanes] = right[rows].astype(BF16)


def pick_columns(first, own, other):
    return jnp.where(
        first, jnp.concatenate([own, other], axis=1), jnp.concatenate([other, own], axis=1)
    )


def first_kernel(meta, own, other, gain, weight, *refs):
    stream, normed_out, *messages, table = refs
    first = meta[0] == 0
    rows, cols, channels = own.shape
    width = GROUP * 2 * cols
    factors = column_of(gain[...], channels)
    table[...] = weight[...].astype(F32).T
    weights = side_weights(table, meta)

    @steps(rows // GROUP)
    def _(step):
        lanes = pl.ds(step * width, width)
        here = pl.ds(step * GROUP, GROUP)
        values = pick_columns(first, own[here].astype(F32), other[here].astype(F32))
        values = values.reshape(width, channels).T
        stream[:, lanes] = values

    @blocks(stream.shape[1])
    def _(lanes):
        normed = norm_rows(stream[:, lanes], factors).astype(BF16)
        normed_out[:, lanes] = normed
        send_sides(normed, weights, messages, lanes)


def gate_of(normed, weight, update):
    channels = normed.shape[0]
    hidden = (weight.shape[2] - channels) // 4
    table = (0.5 * weight[update, :, 4 * hidden :].astype(F32).T).astype(BF16)
    return sigmoid_of_double(jnp.dot(table, normed[...], preferred_element_type=F32))


def chip_masks(bits, column, meta, masks, width):
    dap, sub = meta[1] >> 1, meta[1] & 1
    rows = masks.shape[1]
    values = bits[...].astype(F32)
    column[...] = jnp.broadcast_to(values, (LANES, values.shape[1])).T
    parts = [values[:, b * width : (b + 1) * width] for b in range(2)]
    parts = [jnp.concatenate([p, jnp.zeros((1, LANES - width), F32)], axis=1) for p in parts]
    for k in range(8):
        begin = aligned((dap ^ (k >> 1)) * rows, GROUP)
        masks[k] = column[pl.ds(begin, rows), :] * jnp.where(sub == (k & 1), parts[0], parts[1])


def first_gate_kernel(meta, normed, weight, entry_gain, middle_gain, out_weight, bits, *refs):
    gate, out_weights, middle, factor, weights, masks, table, out_table, square, column = refs
    chip_masks(bits, column, meta, masks, bits.shape[1] // 2)
    gate[...] = gate_of(normed, weight, 0)
    out_table[...] = out_weight[0].astype(F32)
    out_weights[...], middle[...] = output_weights(out_table, square, middle_gain[0:1, :], meta)
    factor[...] = column_of(entry_gain[1:2, :], factor.shape[1])
    table[...] = weight[1, :, : table.shape[0]].astype(F32).T
    weights[...] = side_weights(table, meta)


def second_gate_kernel(meta, normed, weight, middle_gain, out_weight, *refs):
    gate, out_weights, middle, out_table, square = refs
    gate[...] = gate_of(normed, weight, 1)
    out_table[...] = out_weight[1].astype(F32)
    out_weights[...], middle[...] = output_weights(out_table, square, middle_gain[1:2, :], meta)


def spread_group(side, part, masks, begin, pitch, width):
    for c in range(0, part.shape[0], GROUP):
        for i, piece in enumerate(split_group(part[c : c + GROUP], width)):
            side[pl.ds(c * pitch + begin + i, GROUP, stride=pitch), :] = piece * masks[i : i + 1]


def gather_group(total, count, begin, pitch, width, lane):
    joined = []
    for c in range(0, count, GROUP):
        pieces = [
            total[pl.ds(c * pitch + begin + i, GROUP, stride=pitch), :] for i in range(GROUP)
        ]
        joined.append(join_group(pieces, width, lane))
    return jnp.concatenate(joined, axis=0).astype(BF16)


def outgoing_kernel(meta, masks, *refs, rows, width):
    messages, outs = dict(zip(FIRST_ORDER, refs[:8])), refs[8:12]
    left, right, total = refs[12:]
    dap, sub = meta[1] >> 1, meta[1] & 1
    lane = lane_index()
    count = outs[0].shape[0]
    span = 2 * rows
    pitch = span + GROUP

    @steps(rows // GROUP)
    def _(step):
        lanes = pl.ds(step * GROUP * width, GROUP * width)
        for k in range(8):
            values = messages[k][:, lanes].astype(F32)
            bits = masks[k, step * GROUP : (step + 1) * GROUP, :]
            if k < 4:
                begin = (k >> 1) * rows + step * GROUP
                spread_group(left.at[k & 1], values[:count], bits, begin, pitch, width)
                values = values[count:]
            source = dap ^ (k >> 1)
            begin = ((source >> 1) ^ sub) * (count * pitch) + (source & 1) * rows + step * GROUP
            spread_group(right.at[k & 1], values, bits, begin, pitch, width)

    for c in range(count):
        here = pl.ds(c * pitch, span)
        a = jnp.concatenate([left[0, here, :], left[1, here, :]], axis=1).astype(BF16)
        for half in range(2):
            there = pl.ds((half * count + c) * pitch, span)
            b = jnp.concatenate([right[0, there, :], right[1, there, :]], axis=1).astype(BF16)
            total[half, here, 0:width] = lax.dot_general(
                a, b, (((1,), (1,)), ((), ())), preferred_element_type=F32
            )

    @steps(rows // GROUP)
    def _(step):
        lanes = pl.ds(step * GROUP * width, GROUP * width)
        for k in range(4):
            begin = (k >> 1) * rows + step * GROUP
            outs[k][:, lanes] = gather_group(total.at[k & 1], count, begin, pitch, width, lane)


def incoming_kernel(meta, masks, *refs, rows, width):
    messages, outs = dict(zip(SIDES_WITHIN, refs[:4])), refs[4:12]
    left, right, total = refs[12:]
    dap, sub = meta[1] >> 1, meta[1] & 1
    lane = lane_index()
    count = outs[0].shape[0]
    span = 2 * rows
    pitch = span + GROUP
    tall = 2 * width + GROUP

    @steps(rows // GROUP)
    def _(step):
        lanes = pl.ds(step * GROUP * width, GROUP * width)
        for k in range(4):
            values = messages[k][:, lanes].astype(F32)
            bits = masks[k, step * GROUP : (step + 1) * GROUP, :]
            begin = (k >> 1) * rows + step * GROUP
            spread_group(left.at[k & 1], values[:count], bits, begin, pitch, width)
            spread_group(right.at[k & 1], values[count:], bits, begin, pitch, width)

    for c in range(count):
        here = pl.ds(c * pitch, span)
        b = jnp.concatenate([right[0, here, :], right[1, here, :]], axis=1).astype(BF16)
        for block in range(2):
            a = left[block, here, 0:width].astype(BF16)
            product = lax.dot_general(a, b, (((0,), (0,)), ((), ())), preferred_element_type=F32)
            there = pl.ds(c * tall + block * width, width)
            total[0, there, :] = product[:, :LANES]
            total[1, there, :] = product[:, LANES:]

    @steps(rows // GROUP)
    def _(step):
        lanes = pl.ds(step * GROUP * width, GROUP * width)
        for k in range(8):
            target = dap ^ (k >> 1)
            begin = ((target >> 1) ^ sub) * width + (target & 1) * rows + step * GROUP
            outs[k][:, lanes] = gather_group(total.at[k & 1], count, begin, tall, width, lane)


def output_weights(table, square, gain, meta):
    core, chip = meta[0], meta[1]
    mine = table.shape[0] // 2
    size = mine // 4
    starts = [
        side * mine + size * ((chip & 3) ^ k) for side in (core, 1 - core) for k in range(4)
    ]
    square[...] = jnp.broadcast_to(gain, square.shape).T
    return pick_rows(table, starts, size).T.astype(BF16), pick_rows(square, starts, size)


def add_update(own, other, stream, gate, weights, factor, lanes):
    mixed = jnp.concatenate([own[:, lanes].astype(F32), other[:, lanes].astype(F32)], axis=0)
    middle = norm_rows(mixed, factor).astype(BF16)
    return stream[:, lanes] + gate[:, lanes] * jnp.dot(weights, middle, preferred_element_type=F32)


def second_kernel(
    own, other, stream, gate, out_weights, middle, factor, weights, *refs, width
):
    stream_out, normed_out, *messages = refs
    channels = stream.shape[0]
    middles = jnp.concatenate([middle[...]] * (width // channels), axis=1)
    factors = factor[...]

    @blocks(stream.shape[1], width)
    def _(lanes):
        values = add_update(own, other, stream, gate, out_weights[...], middles, lanes)
        stream_out[:, lanes] = values
        normed = norm_rows(values, factors).astype(BF16)
        normed_out[:, lanes] = normed
        send_sides(normed, weights[...], messages, lanes)


def last_scratch(channels, pairs):
    return [pltpu.VMEM((channels, pairs), F32)]


def last_kernel(
    meta, own, other, stream, gate, out_weights, middle, final_gain, expand, shrink, result, total
):
    first = meta[0] == 0
    rows, cols, channels = result.shape
    width = GROUP * 2 * cols
    middles = jnp.concatenate([middle[...]] * (width // channels), axis=1)

    @blocks(stream.shape[1])
    def _(lanes):
        total[:, lanes] = add_update(own, other, stream, gate, out_weights[...], middles, lanes)

    @steps(rows // GROUP)
    def _(step):
        values = total[:, pl.ds(step * width, width)].T.reshape(GROUP, 2 * cols, channels)
        flat = jnp.where(first, values[:, :cols], values[:, cols:]).reshape(GROUP * cols, channels)
        normed = layer_norm(flat, final_gain[...], 1).astype(BF16)
        expanded = jnp.dot(normed, expand[...], preferred_element_type=F32)
        expanded = jnp.maximum(expanded, 0.0).astype(BF16)
        out = flat + jnp.dot(expanded, shrink[...], preferred_element_type=F32)
        result[pl.ds(step * GROUP, GROUP)] = out.astype(BF16).reshape(GROUP, cols, channels)


def call(kernel, outs, scratch, args, scalars=1, flops=0):
    in_specs = [pl.BlockSpec(memory_space=pltpu.SMEM)] * scalars
    in_specs += [pl.BlockSpec(memory_space=pltpu.VMEM)] * (len(args) - scalars)
    moved = sum(a.size * a.dtype.itemsize for a in (*args, *outs))
    return pl.pallas_call(
        kernel,
        out_shape=outs,
        in_specs=in_specs,
        out_specs=[pl.BlockSpec(memory_space=pltpu.VMEM)] * len(outs),
        scratch_shapes=scratch,
        compiler_params=pltpu.CompilerParams(vmem_limit_bytes=40 * 1024 * 1024),
        cost_estimate=pl.CostEstimate(flops=flops, bytes_accessed=moved, transcendentals=0),
    )(*args)


def to_chip(value, distance):
    if distance == 0:
        return value
    pairs = [(device, device ^ (2 * distance)) for device in range(16)]
    return lax.ppermute(value, CHIPS, pairs)


def swap_cores(value):
    return lax.ppermute(value, "pair", [(0, 1), (1, 0)])


def chip_device(
    pair_input,
    residue_mask,
    entry_gain,
    input_weight,
    middle_gain,
    output_weight,
    final_gain,
    expand_weight,
    shrink_weight,
):
    rows, cols, channels = pair_input.shape
    hidden = output_weight.shape[1]
    width = 2 * cols
    pairs = rows * width
    wide = GROUP * width
    dap, sub, core = lax.axis_index("dap"), lax.axis_index("sub"), lax.axis_index("pair")
    meta = jnp.stack([core, dap * 2 + sub]).astype(jnp.int32)
    other_input = swap_cores(pair_input)
    shape = jax.ShapeDtypeStruct
    flat32, flat16 = shape((channels, pairs), F32), shape((channels, pairs), BF16)
    part = hidden // 8
    sides, rights = shape((2 * part, pairs), BF16), shape((part, pairs), BF16)
    span, tall = 2 * rows + GROUP, 2 * width + GROUP

    square32, square16 = shape((channels, channels), F32), shape((hidden, channels), BF16)
    side_weight = shape((2 * hidden, channels), BF16)
    stream, normed, *messages = call(
        first_kernel,
        [flat32, flat16] + [sides] * 4 + [rights] * 4,
        [pltpu.VMEM((4 * hidden, channels), F32)],
        (meta, pair_input, other_input, entry_gain[0:1], input_weight[0, :, : 4 * hidden]),
    )
    arrived = [to_chip(messages[k], k) for k in FIRST_ORDER]
    length = residue_mask.shape[0]
    gate, out_weights, middle, factor, weights, masks = call(
        first_gate_kernel,
        [flat32, square16, square32, square32, side_weight, shape((8, rows, LANES), F32)],
        [
            pltpu.VMEM((4 * hidden, channels), F32),
            pltpu.VMEM((hidden, channels), F32),
            pltpu.VMEM((hidden, LANES), F32),
            pltpu.VMEM((length, LANES), F32),
        ],
        (
            meta, normed, input_weight, entry_gain, middle_gain, output_weight,
            residue_mask.reshape(1, length),
        ),
    )
    sums = call(
        functools.partial(outgoing_kernel, rows=rows, width=width),
        [rights] * 4,
        [
            pltpu.VMEM((2, part * span, LANES), F32),
            pltpu.VMEM((2, 2 * part * span, LANES), F32),
            pltpu.VMEM((2, part * span, LANES), F32),
        ],
        (meta, masks, *arrived),
    )
    returned = [to_chip(sums[k], k) for k in WITHIN_HALF]
    own = jnp.concatenate(returned[::-1], axis=0)
    other = swap_cores(own)
    stream, normed, *messages = call(
        functools.partial(second_kernel, width=wide),
        [flat32, flat16] + [sides] * 4,
        [],
        (own, other, stream, gate, out_weights, middle, factor, weights),
        0,
    )
    arrived = [to_chip(messages[k], k) for k in SIDES_WITHIN]
    gate, out_weights, middle = call(
        second_gate_kernel,
        [flat32, square16, square32],
        [pltpu.VMEM((hidden, channels), F32), pltpu.VMEM((hidden, LANES), F32)],
        (meta, normed, input_weight, middle_gain, output_weight),
    )
    sums = call(
        functools.partial(incoming_kernel, rows=rows, width=width),
        [rights] * 8,
        [
            pltpu.VMEM((2, part * span, LANES), F32),
            pltpu.VMEM((2, part * span, LANES), F32),
            pltpu.VMEM((2, part * tall, LANES), F32),
        ],
        (meta, masks, *arrived),
    )
    returned = {k: to_chip(sums[k], k) for k in LAST_ORDER}
    near = jnp.concatenate([returned[k] for k in range(4)], axis=0)
    far = jnp.concatenate([returned[4 + k] for k in range(4)], axis=0)
    own = (near.astype(F32) + far.astype(F32)).astype(BF16)
    other = swap_cores(own)
    (result,) = call(
        last_kernel,
        [shape((rows, cols, channels), BF16)],
        last_scratch(channels, pairs),
        (
            meta, own, other, stream, gate, out_weights, middle,
            final_gain.reshape(1, channels), expand_weight, shrink_weight,
        ),
    )
    return result


def by_chips(mesh, pair_input, output_weight):
    sizes = dict(mesh.shape)
    rows = pair_input.shape[0] // (sizes["grp"] * sizes["dap"])
    cols = pair_input.shape[1] // (sizes["sub"] * sizes["pair"])
    return (
        (sizes["dap"], sizes["sub"], sizes["pair"]) == (4, 2, 2)
        and pair_input.shape[2] == LANES
        and output_weight.shape[1] == LANES
        and rows == cols
        and rows % GROUP == 0
        and 2 * cols <= LANES
        and GROUP * 2 * cols % LANES == 0
    )


def solution(mesh):
    placed = (P(("grp", "dap"), ("sub", "pair"), None), P("grp"), P(), P(), P(), P(), P(), P(), P())

    def run(*args):
        fits = by_chips(mesh, args[0], args[5])
        return jax.shard_map(
            chip_device if fits else general_device,
            mesh=mesh,
            in_specs=placed,
            out_specs=P(("grp", "dap"), ("sub", "pair"), None),
            check_vma=False,
        )(*args)

    return run
```

```python
import functools

import jax
import jax.numpy as jnp
from jax import lax
from jax.experimental import pallas as pl
from jax.experimental.pallas import tpu as pltpu
from jax.sharding import PartitionSpec as P

F32 = jnp.float32
BF16 = jnp.bfloat16
LANES = 128
GROUP = 8
CHIPS = ("dap", "sub", "pair")


def layer_norm(values, factor, dimension):
    average = jnp.mean(values, axis=dimension, keepdims=True)
    centred = values - average
    variance = jnp.mean(centred * centred, axis=dimension, keepdims=True)
    return centred * lax.rsqrt(variance + 1e-05) * factor


def spread_rows(left_side, right_side):
    return (
        lax.all_to_all(left_side, ("sub", "pair"), split_axis=0, concat_axis=2, tiled=True),
        lax.all_to_all(right_side, ("sub", "pair"), split_axis=0, concat_axis=2, tiled=True),
    )


def return_rows(mixed_sum):
    return lax.all_to_all(mixed_sum, ("sub", "pair"), split_axis=2, concat_axis=0, tiled=True)


def outgoing_rows(left_side, right_side):
    left_wide, right_wide = spread_rows(left_side, right_side)
    summed = jnp.einsum(
        "cik,cjk->cij",
        left_wide,
        lax.all_gather(right_wide, "dap", axis=1, tiled=True),
        preferred_element_type=jnp.float32,
    )
    return return_rows(summed.astype(jnp.bfloat16))


def incoming_rows(left_side, right_side):
    left_wide, right_wide = spread_rows(left_side, right_side)
    flipped = lax.all_to_all(left_wide, "dap", split_axis=2, concat_axis=1, tiled=True)
    summed = jnp.einsum(
        "cki,ckj->cij",
        flipped,
        lax.all_gather(right_wide, "dap", axis=1, tiled=True),
        preferred_element_type=jnp.float32,
    )
    return return_rows(summed.astype(jnp.bfloat16))


def triangle_update(
    stream, pair_mask, entry_gain, input_weight, middle_gain, output_weight, incoming
):
    row_count, col_count, channels = stream.shape
    hidden = output_weight.shape[0]
    normed = (
        layer_norm(stream, entry_gain, 2)
        .astype(jnp.bfloat16)
        .reshape(row_count * col_count, channels)
    )
    projected = lax.dot_general(
        input_weight[:, : 4 * hidden],
        normed,
        (((0,), (1,)), ((), ())),
        preferred_element_type=jnp.float32,
    )
    projected = projected.reshape(4 * hidden, row_count, col_count)
    left_side = (
        pair_mask * jax.nn.sigmoid(projected[hidden : 2 * hidden]) * projected[:hidden]
    ).astype(jnp.bfloat16)
    right_side = (
        pair_mask * jax.nn.sigmoid(projected[3 * hidden :]) * projected[2 * hidden : 3 * hidden]
    ).astype(jnp.bfloat16)
    gate_vals = jax.nn.sigmoid(
        jnp.dot(normed, input_weight[:, 4 * hidden :], preferred_element_type=jnp.float32)
    )
    mixed_sum = (
        incoming_rows(left_side, right_side) if incoming else outgoing_rows(left_side, right_side)
    )
    middle = layer_norm(mixed_sum.astype(jnp.float32), middle_gain[:, None, None], 0).astype(
        jnp.bfloat16
    )
    middle = middle.reshape(hidden, row_count * col_count)
    output = lax.dot_general(
        middle, output_weight, (((0,), (0,)), ((), ())), preferred_element_type=jnp.float32
    )
    return stream + (gate_vals * output).reshape(row_count, col_count, channels)


def general_device(
    pair_input,
    residue_mask,
    entry_gain,
    input_weight,
    middle_gain,
    output_weight,
    final_gain,
    expand_weight,
    shrink_weight,
):
    row_count, col_count, channels = pair_input.shape
    row_offset = lax.axis_index("dap") * row_count
    col_offset = lax.axis_index(("sub", "pair")) * col_count
    row_mask = lax.dynamic_slice_in_dim(residue_mask, row_offset, row_count).astype(jnp.float32)
    col_mask = lax.dynamic_slice_in_dim(residue_mask, col_offset, col_count).astype(jnp.float32)
    pair_mask = row_mask[:, None] * col_mask[None, :]
    stream = pair_input.astype(jnp.float32)
    for update_id in range(2):
        stream = triangle_update(
            stream,
            pair_mask,
            entry_gain[update_id],
            input_weight[update_id],
            middle_gain[update_id],
            output_weight[update_id],
            update_id == 1,
        )
    flat = stream.reshape(row_count * col_count, channels)
    normed = layer_norm(flat, final_gain, 1).astype(jnp.bfloat16)
    expanded = jax.nn.relu(
        jnp.dot(normed, expand_weight, preferred_element_type=jnp.float32)
    ).astype(jnp.bfloat16)
    result = flat + jnp.dot(expanded, shrink_weight, preferred_element_type=jnp.float32)
    return result.astype(jnp.bfloat16).reshape(row_count, col_count, channels)


FIRST_ORDER = (4, 5, 2, 6, 3, 7, 1, 0)
LAST_ORDER = (4, 2, 5, 3, 6, 1, 7, 0)
WITHIN_HALF = (3, 2, 1, 0)
SIDES_WITHIN = (2, 1, 3, 0)


def aligned(start, size):
    return start if isinstance(start, int) else pl.multiple_of(start, size)


def steps(count):
    def run(body):
        for step in range(count):
            body(step)

    return run


def blocks(count, size=2 * LANES):
    def run(body):
        for begin in range(0, count, size):
            body(slice(begin, min(begin + size, count)))

    return run


def sigmoid_of_double(values):
    return 0.5 * jnp.tanh(values) + 0.5


def norm_rows(values, factor):
    return jnp.concatenate(
        [
            norm_block(values[:, b : b + LANES], factor[:, :LANES])
            for b in range(0, values.shape[1], LANES)
        ],
        axis=1,
    )


def norm_block(values, factor):
    average = jnp.mean(values, axis=0, keepdims=True)
    centred = values - average
    variance = jnp.mean(centred * centred, axis=0, keepdims=True)
    return centred * lax.rsqrt(variance + 1e-05) * factor


def column_of(gain_row, width):
    square = jnp.broadcast_to(gain_row, (gain_row.shape[1], gain_row.shape[1])).T
    return jnp.concatenate([square] * (width // square.shape[1]), axis=1)


def lane_index():
    return lax.broadcasted_iota(jnp.int32, (GROUP, LANES), 1)


def split_group(chunk, width):
    lane = lane_index()
    pieces = []
    for row in range(GROUP):
        first, offset = divmod(row * width, LANES)
        piece = chunk[:, first * LANES : (first + 1) * LANES]
        if offset:
            piece = pltpu.roll(piece, LANES - offset, 1)
            if offset + width > LANES:
                after = chunk[:, (first + 1) * LANES : (first + 2) * LANES]
                after = pltpu.roll(after, LANES - offset, 1)
                piece = jnp.where(lane < LANES - offset, piece, after)
        pieces.append(piece)
    return pieces


def join_group(pieces, width, lane):
    parts = []
    for part in range(GROUP * width // LANES):
        begin = part * LANES
        value = None
        for row in range(begin // width, (begin + LANES - 1) // width + 1):
            shift = row * width - begin
            piece = pieces[row]
            if shift % LANES:
                piece = pltpu.roll(piece, shift % LANES, 1)
            value = piece if value is None else jnp.where(lane >= shift, piece, value)
        parts.append(value)
    return jnp.concatenate(parts, axis=1)


def pick_rows(table, starts, size):
    return jnp.concatenate(
        [table[pl.ds(aligned(start, GROUP), size), :] for start in starts], axis=0
    )


def side_weights(table, meta):
    core, chip = meta[0], meta[1]
    hidden = table.shape[0] // 4
    mine = hidden // 2
    size = mine // 4
    picked = []
    for base in range(4):
        starts = [base * hidden + core * mine + size * ((chip & 3) ^ k) for k in range(4)]
        picked.append(pick_rows(table, starts, size))
    return (0.5 * jnp.concatenate(picked, axis=0)).astype(BF16)


def send_sides(normed, weights, messages, lanes):
    quarter = weights.shape[0] // 4
    projected = jnp.dot(weights, normed, preferred_element_type=F32)
    left = (jnp.tanh(projected[quarter : 2 * quarter]) + 1.0) * projected[:quarter]
    right = (jnp.tanh(projected[3 * quarter :]) + 1.0) * projected[2 * quarter : 3 * quarter]
    size = quarter // 4
    for k in range(4):
        rows = slice(k * size, (k + 1) * size)
        messages[k][:, lanes] = jnp.concatenate([left[rows], right[rows]], axis=0).astype(BF16)
        if len(messages) > 4:
            messages[4 + k][:, lanes] = right[rows].astype(BF16)


def pick_columns(first, own, other):
    return jnp.where(
        first, jnp.concatenate([own, other], axis=1), jnp.concatenate([other, own], axis=1)
    )


def first_kernel(meta, own, other, gain, weight, *refs):
    stream, normed_out, *messages, table = refs
    first = meta[0] == 0
    rows, cols, channels = own.shape
    width = GROUP * 2 * cols
    factors = column_of(gain[...], channels)
    table[...] = weight[...].astype(F32).T
    weights = side_weights(table, meta)

    @steps(rows // GROUP)
    def _(step):
        lanes = pl.ds(step * width, width)
        here = pl.ds(step * GROUP, GROUP)
        values = pick_columns(first, own[here].astype(F32), other[here].astype(F32))
        values = values.reshape(width, channels).T
        stream[:, lanes] = values

    @blocks(stream.shape[1])
    def _(lanes):
        normed = norm_rows(stream[:, lanes], factors).astype(BF16)
        normed_out[:, lanes] = normed
        send_sides(normed, weights, messages, lanes)


def gate_of(normed, weight, update):
    channels = normed.shape[0]
    hidden = (weight.shape[2] - channels) // 4
    table = (0.5 * weight[update, :, 4 * hidden :].astype(F32).T).astype(BF16)
    return sigmoid_of_double(jnp.dot(table, normed[...], preferred_element_type=F32))


def chip_masks(bits, column, meta, masks, width):
    dap, sub = meta[1] >> 1, meta[1] & 1
    rows = masks.shape[1]
    values = bits[...].astype(F32)
    column[...] = jnp.broadcast_to(values, (LANES, values.shape[1])).T
    parts = [values[:, b * width : (b + 1) * width] for b in range(2)]
    parts = [jnp.concatenate([p, jnp.zeros((1, LANES - width), F32)], axis=1) for p in parts]
    for k in range(8):
        begin = aligned((dap ^ (k >> 1)) * rows, GROUP)
        masks[k] = column[pl.ds(begin, rows), :] * jnp.where(sub == (k & 1), parts[0], parts[1])


def first_gate_kernel(meta, normed, weight, entry_gain, middle_gain, out_weight, bits, *refs):
    gate, out_weights, middle, factor, weights, masks, table, out_table, square, column = refs
    chip_masks(bits, column, meta, masks, bits.shape[1] // 2)
    gate[...] = gate_of(normed, weight, 0)
    out_table[...] = out_weight[0].astype(F32)
    out_weights[...], middle[...] = output_weights(out_table, square, middle_gain[0:1, :], meta)
    factor[...] = column_of(entry_gain[1:2, :], factor.shape[1])
    table[...] = weight[1, :, : table.shape[0]].astype(F32).T
    weights[...] = side_weights(table, meta)


def second_gate_kernel(meta, normed, weight, middle_gain, out_weight, *refs):
    gate, out_weights, middle, out_table, square = refs
    gate[...] = gate_of(normed, weight, 1)
    out_table[...] = out_weight[1].astype(F32)
    out_weights[...], middle[...] = output_weights(out_table, square, middle_gain[1:2, :], meta)


def spread_group(side, part, masks, begin, pitch, width):
    for c in range(0, part.shape[0], GROUP):
        for i, piece in enumerate(split_group(part[c : c + GROUP], width)):
            side[pl.ds(c * pitch + begin + i, GROUP, stride=pitch), :] = piece * masks[i : i + 1]


def gather_group(total, count, begin, pitch, width, lane):
    joined = []
    for c in range(0, count, GROUP):
        pieces = [
            total[pl.ds(c * pitch + begin + i, GROUP, stride=pitch), :] for i in range(GROUP)
        ]
        joined.append(join_group(pieces, width, lane))
    return jnp.concatenate(joined, axis=0).astype(BF16)


def outgoing_kernel(meta, masks, *refs, rows, width):
    messages, outs = dict(zip(FIRST_ORDER, refs[:8])), refs[8:12]
    left, right, total = refs[12:]
    dap, sub = meta[1] >> 1, meta[1] & 1
    lane = lane_index()
    count = outs[0].shape[0]
    span = 2 * rows
    pitch = span + GROUP

    @steps(rows // GROUP)
    def _(step):
        lanes = pl.ds(step * GROUP * width, GROUP * width)
        for k in range(8):
            values = messages[k][:, lanes].astype(F32)
            bits = masks[k, step * GROUP : (step + 1) * GROUP, :]
            if k < 4:
                begin = (k >> 1) * rows + step * GROUP
                spread_group(left.at[k & 1], values[:count], bits, begin, pitch, width)
                values = values[count:]
            source = dap ^ (k >> 1)
            begin = ((source >> 1) ^ sub) * (count * pitch) + (source & 1) * rows + step * GROUP
            spread_group(right.at[k & 1], values, bits, begin, pitch, width)

    for c in range(count):
        here = pl.ds(c * pitch, span)
        a = jnp.concatenate([left[0, here, :], left[1, here, :]], axis=1).astype(BF16)
        for half in range(2):
            there = pl.ds((half * count + c) * pitch, span)
            b = jnp.concatenate([right[0, there, :], right[1, there, :]], axis=1).astype(BF16)
            total[half, here, 0:width] = lax.dot_general(
                a, b, (((1,), (1,)), ((), ())), preferred_element_type=F32
            )

    @steps(rows // GROUP)
    def _(step):
        lanes = pl.ds(step * GROUP * width, GROUP * width)
        for k in range(4):
            begin = (k >> 1) * rows + step * GROUP
            outs[k][:, lanes] = gather_group(total.at[k & 1], count, begin, pitch, width, lane)


def incoming_kernel(meta, masks, *refs, rows, width):
    messages, outs = dict(zip(SIDES_WITHIN, refs[:4])), refs[4:12]
    left, right, total = refs[12:]
    dap, sub = meta[1] >> 1, meta[1] & 1
    lane = lane_index()
    count = outs[0].shape[0]
    span = 2 * rows
    pitch = span + GROUP
    tall = 2 * width + GROUP

    @steps(rows // GROUP)
    def _(step):
        lanes = pl.ds(step * GROUP * width, GROUP * width)
        for k in range(4):
            values = messages[k][:, lanes].astype(F32)
            bits = masks[k, step * GROUP : (step + 1) * GROUP, :]
            begin = (k >> 1) * rows + step * GROUP
            spread_group(left.at[k & 1], values[:count], bits, begin, pitch, width)
            spread_group(right.at[k & 1], values[count:], bits, begin, pitch, width)

    for c in range(count):
        here = pl.ds(c * pitch, span)
        b = jnp.concatenate([right[0, here, :], right[1, here, :]], axis=1).astype(BF16)
        for block in range(2):
            a = left[block, here, 0:width].astype(BF16)
            product = lax.dot_general(a, b, (((0,), (0,)), ((), ())), preferred_element_type=F32)
            there = pl.ds(c * tall + block * width, width)
            total[0, there, :] = product[:, :LANES]
            total[1, there, :] = product[:, LANES:]

    @steps(rows // GROUP)
    def _(step):
        lanes = pl.ds(step * GROUP * width, GROUP * width)
        for k in range(8):
            target = dap ^ (k >> 1)
            begin = ((target >> 1) ^ sub) * width + (target & 1) * rows + step * GROUP
            outs[k][:, lanes] = gather_group(total.at[k & 1], count, begin, tall, width, lane)


def add_halves_kernel(*refs):
    parts, out = dict(zip(LAST_ORDER, refs[:8])), refs[8]
    size = parts[0].shape[0]
    for k in range(4):
        value = parts[k][...].astype(F32) + parts[4 + k][...].astype(F32)
        out[k * size : (k + 1) * size, :] = value.astype(BF16)


def output_weights(table, square, gain, meta):
    core, chip = meta[0], meta[1]
    mine = table.shape[0] // 2
    size = mine // 4
    starts = [
        side * mine + size * ((chip & 3) ^ k) for side in (core, 1 - core) for k in range(4)
    ]
    square[...] = jnp.broadcast_to(gain, square.shape).T
    return pick_rows(table, starts, size).T.astype(BF16), pick_rows(square, starts, size)


def add_update(own, other, stream, gate, weights, factor, lanes):
    mixed = jnp.concatenate([own[:, lanes].astype(F32), other[:, lanes].astype(F32)], axis=0)
    middle = norm_rows(mixed, factor).astype(BF16)
    return stream[:, lanes] + gate[:, lanes] * jnp.dot(weights, middle, preferred_element_type=F32)


def second_kernel(
    own, other, stream, gate, out_weights, middle, factor, weights, *refs, width
):
    stream_out, normed_out, *messages = refs
    channels = stream.shape[0]
    middles = jnp.concatenate([middle[...]] * (width // channels), axis=1)
    factors = factor[...]

    @blocks(stream.shape[1], width)
    def _(lanes):
        values = add_update(own, other, stream, gate, out_weights[...], middles, lanes)
        stream_out[:, lanes] = values
        normed = norm_rows(values, factors).astype(BF16)
        normed_out[:, lanes] = normed
        send_sides(normed, weights[...], messages, lanes)


def last_scratch(channels, pairs):
    return [pltpu.VMEM((channels, pairs), F32)]


def last_kernel(
    meta, own, other, stream, gate, out_weights, middle, final_gain, expand, shrink, result, total
):
    first = meta[0] == 0
    rows, cols, channels = result.shape
    width = GROUP * 2 * cols
    middles = jnp.concatenate([middle[...]] * (width // channels), axis=1)

    @blocks(stream.shape[1])
    def _(lanes):
        total[:, lanes] = add_update(own, other, stream, gate, out_weights[...], middles, lanes)

    @steps(rows // GROUP)
    def _(step):
        values = total[:, pl.ds(step * width, width)].T.reshape(GROUP, 2 * cols, channels)
        flat = jnp.where(first, values[:, :cols], values[:, cols:]).reshape(GROUP * cols, channels)
        normed = layer_norm(flat, final_gain[...], 1).astype(BF16)
        expanded = jnp.dot(normed, expand[...], preferred_element_type=F32)
        expanded = jnp.maximum(expanded, 0.0).astype(BF16)
        out = flat + jnp.dot(expanded, shrink[...], preferred_element_type=F32)
        result[pl.ds(step * GROUP, GROUP)] = out.astype(BF16).reshape(GROUP, cols, channels)


def call(kernel, outs, scratch, args, scalars=1, flops=0):
    in_specs = [pl.BlockSpec(memory_space=pltpu.SMEM)] * scalars
    in_specs += [pl.BlockSpec(memory_space=pltpu.VMEM)] * (len(args) - scalars)
    moved = sum(a.size * a.dtype.itemsize for a in (*args, *outs))
    return pl.pallas_call(
        kernel,
        out_shape=outs,
        in_specs=in_specs,
        out_specs=[pl.BlockSpec(memory_space=pltpu.VMEM)] * len(outs),
        scratch_shapes=scratch,
        compiler_params=pltpu.CompilerParams(vmem_limit_bytes=40 * 1024 * 1024),
        cost_estimate=pl.CostEstimate(flops=flops, bytes_accessed=moved, transcendentals=0),
    )(*args)


def to_chip(value, distance):
    if distance == 0:
        return value
    pairs = [(device, device ^ (2 * distance)) for device in range(16)]
    return lax.ppermute(value, CHIPS, pairs)


def swap_cores(value):
    return lax.ppermute(value, "pair", [(0, 1), (1, 0)])


def chip_device(
    pair_input,
    residue_mask,
    entry_gain,
    input_weight,
    middle_gain,
    output_weight,
    final_gain,
    expand_weight,
    shrink_weight,
):
    rows, cols, channels = pair_input.shape
    hidden = output_weight.shape[1]
    width = 2 * cols
    pairs = rows * width
    wide = GROUP * width
    dap, sub, core = lax.axis_index("dap"), lax.axis_index("sub"), lax.axis_index("pair")
    meta = jnp.stack([core, dap * 2 + sub]).astype(jnp.int32)
    other_input = swap_cores(pair_input)
    shape = jax.ShapeDtypeStruct
    flat32, flat16 = shape((channels, pairs), F32), shape((channels, pairs), BF16)
    part = hidden // 8
    sides, rights = shape((2 * part, pairs), BF16), shape((part, pairs), BF16)
    span, tall = 2 * rows + GROUP, 2 * width + GROUP

    square32, square16 = shape((channels, channels), F32), shape((hidden, channels), BF16)
    side_weight = shape((2 * hidden, channels), BF16)
    stream, normed, *messages = call(
        first_kernel,
        [flat32, flat16] + [sides] * 4 + [rights] * 4,
        [pltpu.VMEM((4 * hidden, channels), F32)],
        (meta, pair_input, other_input, entry_gain[0:1], input_weight[0, :, : 4 * hidden]),
    )
    arrived = [to_chip(messages[k], k) for k in FIRST_ORDER]
    length = residue_mask.shape[0]
    gate, out_weights, middle, factor, weights, masks = call(
        first_gate_kernel,
        [flat32, square16, square32, square32, side_weight, shape((8, rows, LANES), F32)],
        [
            pltpu.VMEM((4 * hidden, channels), F32),
            pltpu.VMEM((hidden, channels), F32),
            pltpu.VMEM((hidden, LANES), F32),
            pltpu.VMEM((length, LANES), F32),
        ],
        (
            meta, normed, input_weight, entry_gain, middle_gain, output_weight,
            residue_mask.reshape(1, length),
        ),
    )
    sums = call(
        functools.partial(outgoing_kernel, rows=rows, width=width),
        [rights] * 4,
        [
            pltpu.VMEM((2, part * span, LANES), F32),
            pltpu.VMEM((2, 2 * part * span, LANES), F32),
            pltpu.VMEM((2, part * span, LANES), F32),
        ],
        (meta, masks, *arrived),
    )
    returned = [to_chip(sums[k], k) for k in WITHIN_HALF]
    own = jnp.concatenate(returned[::-1], axis=0)
    other = swap_cores(own)
    stream, normed, *messages = call(
        functools.partial(second_kernel, width=wide),
        [flat32, flat16] + [sides] * 4,
        [],
        (own, other, stream, gate, out_weights, middle, factor, weights),
        0,
    )
    arrived = [to_chip(messages[k], k) for k in SIDES_WITHIN]
    gate, out_weights, middle = call(
        second_gate_kernel,
        [flat32, square16, square32],
        [pltpu.VMEM((hidden, channels), F32), pltpu.VMEM((hidden, LANES), F32)],
        (meta, normed, input_weight, middle_gain, output_weight),
    )
    sums = call(
        functools.partial(incoming_kernel, rows=rows, width=width),
        [rights] * 8,
        [
            pltpu.VMEM((2, part * span, LANES), F32),
            pltpu.VMEM((2, part * span, LANES), F32),
            pltpu.VMEM((2, part * tall, LANES), F32),
        ],
        (meta, masks, *arrived),
    )
    returned = [to_chip(sums[k], k) for k in LAST_ORDER]
    (own,) = call(add_halves_kernel, [shape((4 * part, pairs), BF16)], [], returned, 0)
    other = swap_cores(own)
    (result,) = call(
        last_kernel,
        [shape((rows, cols, channels), BF16)],
        last_scratch(channels, pairs),
        (
            meta, own, other, stream, gate, out_weights, middle,
            final_gain.reshape(1, channels), expand_weight, shrink_weight,
        ),
    )
    return result


def by_chips(mesh, pair_input, output_weight):
    sizes = dict(mesh.shape)
    rows = pair_input.shape[0] // (sizes["grp"] * sizes["dap"])
    cols = pair_input.shape[1] // (sizes["sub"] * sizes["pair"])
    return (
        (sizes["dap"], sizes["sub"], sizes["pair"]) == (4, 2, 2)
        and pair_input.shape[2] == LANES
        and output_weight.shape[1] == LANES
        and rows == cols
        and rows % GROUP == 0
        and 2 * cols <= LANES
        and GROUP * 2 * cols % LANES == 0
    )


def solution(mesh):
    placed = (P(("grp", "dap"), ("sub", "pair"), None), P("grp"), P(), P(), P(), P(), P(), P(), P())

    def run(*args):
        fits = by_chips(mesh, args[0], args[5])
        return jax.shard_map(
            chip_device if fits else general_device,
            mesh=mesh,
            in_specs=placed,
            out_specs=P(("grp", "dap"), ("sub", "pair"), None),
            check_vma=False,
        )(*args)

    return run
```
